512 devices in a mesh: vintage: 2 (over core), freq: 4 (over x), tile: 64 (over z, y).
Axes of the slice: x: 4, y: 4, z: 16, core: 2. Of those that a mesh axis runs over, the one named last changes fastest.
Arguments:
- observed: bfloat16 [2, 64, 8, 512, 1024], P('vintage', 'tile', 'freq'), parts along dimension 2, may hold values from -6 to 6
- common_left: bfloat16 [1024, 64, 256], P('freq', 'tile'), parts along dimension 0, may hold values from -1.1953125 to 1.1953125
- common_right: bfloat16 [1024, 64, 256], P('freq', 'tile'), parts along dimension 0, may hold values from -1.1953125 to 1.1953125
- innov_left: bfloat16 [2, 1024, 64, 256], P('vintage', 'freq', 'tile'), parts along dimension 1, may hold values from -0.8984375 to 0.8984375
- innov_right: bfloat16 [2, 1024, 64, 256], P('vintage', 'freq', 'tile'), parts along dimension 1, may hold values from -0.8984375 to 0.8984375
- tile_block_pairs: int32 [2, 64, 8, 2], P(None, None, 'freq'), parts along dimension 2, may hold values from 0 to 31
- live: int32 [2, 64, 8], P(None, None, 'freq'), parts along dimension 2, may hold values from 0 to 1, as said below
- row_mask: int32 [2, 64, 8, 512], P('vintage', 'tile', 'freq'), parts along dimension 2, may hold values 0 or 1
- col_mask: int32 [2, 64, 8, 512], P('vintage', 'tile', 'freq'), parts along dimension 2, may hold values 0 or 1
Outputs:
- new_common_left: float32 [1024, 64, 256], P('freq', 'tile'), parts along dimension 0
- new_common_right: float32 [1024, 64, 256], P('freq', 'tile'), parts along dimension 0
- new_innov_left: float32 [2, 1024, 64, 256], P('vintage', 'freq', 'tile'), parts along dimension 1
- new_innov_right: float32 [2, 1024, 64, 256], P('vintage', 'freq', 'tile'), parts along dimension 1
The draws below stay inside these ranges and needn't reach their ends.
There are 4 independent parts, one for each index of `freq`. The reference program is written for one: setup_inputs(seed, part) draws one part's arguments, and reference() takes and returns one part's arrays. A program takes and returns all parts, laid end to end along the dimension named above; each array names one. Nothing has to cross between parts.
Inputs may be any that keep to these rules, and one draw needn't show every extreme that they name: Each device holds 1 to 2 live slots, the live ones first; in each vintage some device has all 2 live.
All inputs are finite; a program needn't handle non-finite values. No bound on the sum of `row_mask` or of `col_mask` on one device may be relied on, other than what follows from the above.
Results may differ from the reference program's by a relative error of at most 0.0041.
Values may be sent and summed in bfloat16 or wider, within the bound.
A program may use at most 64 MiB of HBM per device.

```python
import jax
import jax.numpy as jnp
from jax import lax

N = 16384
TILE_EXTENT = 512
SLOTS = 2
W = 256
BLOCKS = 32
ROWS_DEV = 256
N_TILE = 64


def draw_live(key, part):
    key = jax.random.fold_in(key, 7)
    first_key, second_key = jax.random.split(key)
    counts = jax.random.randint(first_key, (2, N_TILE), 1, SLOTS + 1)
    full_at = jax.random.randint(second_key, (2, 1), 0, N_TILE)
    counts = jnp.where(jnp.arange(N_TILE)[None, :] == full_at, SLOTS, counts)
    return (jnp.arange(SLOTS)[None, None, :] < counts[:, :, None]).astype(jnp.int32)


def plant(result, own_key, least, largest):
    longest = result.shape.index(max(result.shape))
    spots = []
    for shift in (0, 1):
        where = [jax.random.randint(jax.random.fold_in(own_key, axis), (), 0, length) for axis, length in enumerate(result.shape)]
        where[longest] = (where[longest] + shift) % result.shape[longest]
        spots.append(tuple(where))
    return result.at[spots[0]].set(least).at[spots[1]].set(largest)


def steps_of(stream_key, shape, shards, low, top_value):
    level = 1.0
    for dim, blocks in shards:
        heights = jax.random.uniform(jax.random.fold_in(jax.random.fold_in(stream_key, 6), dim), (blocks,), jnp.float32, low / len(shards), top_value / len(shards))
        level = level * jnp.repeat(jnp.exp(heights), shape[dim] // blocks).reshape((-1,) + (1,) * (len(shape) - 1 - dim))
    return level


def centred(stream_key, shape, deviation, reach, pieces=(), kind=jnp.bfloat16):
    loudness = steps_of(stream_key, shape, pieces, -0.22, 0.18) if pieces else 1.0
    array = jax.random.normal(stream_key, shape, jnp.float32) * deviation * loudness
    return jnp.minimum(jnp.maximum(array, -reach), reach).astype(kind)


def setup_inputs(seed: int = 0, part: int = 0) -> dict:
    keys = jax.random.split(jax.random.key(seed), 10)
    part_splits = jax.random.split(jax.random.fold_in(keys[9], part), 10)
    return {
        "observed": centred(part_splits[0], (2, N_TILE, SLOTS, TILE_EXTENT, 2 * TILE_EXTENT), 1.0, 6.0, ((0, 2), (1, 64))),
        "common_left": centred(part_splits[1], (ROWS_DEV, N_TILE, W), 0.2, 1.1953125, ((1, 64),)),
        "common_right": centred(part_splits[2], (ROWS_DEV, N_TILE, W), 0.2, 1.1953125, ((1, 64),)),
        "innov_left": centred(part_splits[3], (2, ROWS_DEV, N_TILE, W), 0.15, 0.8984375, ((0, 2), (2, 64))),
        "innov_right": centred(part_splits[4], (2, ROWS_DEV, N_TILE, W), 0.15, 0.8984375, ((0, 2), (2, 64))),
        "tile_block_pairs": plant(jax.random.randint(part_splits[5], (2, N_TILE, SLOTS, 2), 0, BLOCKS), jax.random.fold_in(part_splits[5], 1), 0, BLOCKS - 1).astype(jnp.int32),
        "live": draw_live(jax.random.fold_in(jax.random.fold_in(keys[9], part), 71), part),
        "row_mask": plant((jax.random.randint(part_splits[7], (2, N_TILE, SLOTS, TILE_EXTENT), 0, 4) < 3).astype(jnp.int32), jax.random.fold_in(part_splits[7], 1), 0, 1),
        "col_mask": plant((jax.random.randint(part_splits[8], (2, N_TILE, SLOTS, TILE_EXTENT), 0, 4) < 3).astype(jnp.int32), jax.random.fold_in(part_splits[8], 1), 0, 1),
    }


step_size = 8.0
shrink = 0.5


def tile_terms(left_factor_block, right_factor_block, observed_tile_values, row_retained, column_retained, active_flag):
    half = left_factor_block.shape[1] // 2
    tile_len = left_factor_block.shape[0]
    s_real = jnp.concatenate([right_factor_block[:, :half], -right_factor_block[:, half:]], axis=1)
    s_imag = jnp.concatenate([right_factor_block[:, half:], right_factor_block[:, :half]], axis=1)
    stacked = jnp.concatenate([s_real, s_imag], axis=0)
    predicted = lax.dot_general(left_factor_block, stacked, (((1,), (1,)), ((), ())), preferred_element_type=jnp.float32)
    weight = row_retained.astype(jnp.float32)[:, None] * column_retained.astype(jnp.float32)[None, :] * active_flag.astype(jnp.float32)
    weight = jnp.concatenate([weight, weight], axis=1)
    misfit = (weight * (predicted - observed_tile_values.astype(jnp.float32))).astype(jnp.bfloat16)
    scale = 1.0 / tile_len
    left_gradient_delta = (jnp.dot(misfit, stacked, preferred_element_type=jnp.float32) * scale).astype(jnp.bfloat16)
    cross = lax.dot_general(misfit, left_factor_block, (((0,), (0,)), ((), ())), preferred_element_type=jnp.float32)
    first = cross[:tile_len]
    second = cross[tile_len:]
    right_gradient_delta = jnp.concatenate([first[:, :half] + second[:, half:], second[:, :half] - first[:, half:]], axis=1)
    right_gradient_delta = (right_gradient_delta * scale).astype(jnp.bfloat16)
    return left_gradient_delta, right_gradient_delta


def reference(observed, common_left, common_right, innov_left, innov_right, tile_block_pairs, live, row_mask, col_mask):
    factor_width = common_left.shape[-1]

    def combine(common, innov):
        joined = (common.astype(jnp.float32)[None] + innov.astype(jnp.float32)).astype(jnp.bfloat16)
        return joined.reshape(2, N, factor_width)

    left_factor_stack = combine(common_left, innov_left)
    right_factor_stack = combine(common_right, innov_right)
    count = 2 * N_TILE * SLOTS
    vintages = (jnp.arange(count, dtype=jnp.int32) // (N_TILE * SLOTS)).astype(jnp.int32)
    items = (vintages, observed.reshape(count, TILE_EXTENT, 2 * TILE_EXTENT),
             tile_block_pairs[..., 0].reshape(count).astype(jnp.int32),
             tile_block_pairs[..., 1].reshape(count).astype(jnp.int32),
             live.reshape(count), row_mask.reshape(count, TILE_EXTENT), col_mask.reshape(count, TILE_EXTENT))

    def accumulate(carry, slot_entry):
        left_gradient_total, right_gradient_total = carry
        vintage_number, observed_tile_values, row_block_number, column_block_number, active_flag, row_retained, column_retained = slot_entry
        zero_gradient = jnp.zeros((), jnp.int32)
        row_begin = (row_block_number * TILE_EXTENT).astype(jnp.int32)
        column_begin = (column_block_number * TILE_EXTENT).astype(jnp.int32)
        left_factor_block = lax.dynamic_slice(left_factor_stack, (vintage_number, row_begin, zero_gradient), (1, TILE_EXTENT, factor_width))[0]
        right_factor_block = lax.dynamic_slice(right_factor_stack, (vintage_number, column_begin, zero_gradient), (1, TILE_EXTENT, factor_width))[0]
        left_gradient_delta, right_gradient_delta = tile_terms(left_factor_block, right_factor_block, observed_tile_values, row_retained, column_retained, active_flag)
        current_left_factor = lax.dynamic_slice(left_gradient_total, (vintage_number, row_begin, zero_gradient), (1, TILE_EXTENT, factor_width))
        left_gradient_total = lax.dynamic_update_slice(left_gradient_total, current_left_factor + left_gradient_delta.astype(jnp.float32)[None], (vintage_number, row_begin, zero_gradient))
        current_right_factor = lax.dynamic_slice(right_gradient_total, (vintage_number, column_begin, zero_gradient), (1, TILE_EXTENT, factor_width))
        right_gradient_total = lax.dynamic_update_slice(right_gradient_total, current_right_factor + right_gradient_delta.astype(jnp.float32)[None], (vintage_number, column_begin, zero_gradient))
        return (left_gradient_total, right_gradient_total), None

    start = jnp.zeros((2, N, factor_width), jnp.float32)
    (left_gradient_total, right_gradient_total), _ = lax.scan(accumulate, (start, start), items)

    def update(common, innov, grads):
        total = (grads[0] + grads[1]).reshape(ROWS_DEV, N_TILE, factor_width)
        own = grads.reshape(2, ROWS_DEV, N_TILE, factor_width)
        innov_f = innov.astype(jnp.float32)
        return common.astype(jnp.float32) - step_size * total, innov_f - step_size * (own + shrink * innov_f)

    new_common_left, new_innov_left = update(common_left, innov_left, left_gradient_total)
    new_common_right, new_innov_right = update(common_right, innov_right, right_gradient_total)
    return (new_common_left, new_common_right, new_innov_left, new_innov_right)
```

```python
import jax
import jax.numpy as jnp
from jax import lax
from jax.experimental import pallas as pl
from jax.experimental.pallas import tpu as pltpu
from jax.sharding import PartitionSpec as P

MESH = pl.DeviceIdType.MESH
BF16, F32 = jnp.bfloat16, jnp.float32

step_size = 8.0
shrink = 0.5

NZ, NY = 16, 4
EXT = 512
NB = 32
HALF = 128
NEAR = 4
FAR = NZ // 2 - NEAR
SIGNS = (1, -1)


def place(rel):
    if abs(rel) == NZ // 2:
        return 0
    far = 2 * (NZ // 2 - abs(rel))
    return far - 1 if rel >= 0 else far


def streams(sign):
    return (0, 1) if sign > 0 else (1, 0)


def far_count(sign, side):
    return FAR if streams(sign)[0] == side else FAR - 1


def dot(a, b, ca=1, cb=0):
    return lax.dot_general(a, b, (((ca,), (cb,)), ((), ())), preferred_element_type=F32)


def kernel(
    pairs,
    live,
    observed,
    common_left,
    common_right,
    innov_left,
    innov_right,
    row_mask,
    col_mask,
    out_common_left,
    out_common_right,
    out_innov_left,
    out_innov_right,
    s,
):
    v = lax.axis_index("vintage")
    t = lax.axis_index("tile")
    z, y = t // NY, t % NY

    def along_z(d):
        return {"tile": lax.rem(z + d + NZ, NZ) * NY + y}

    def along_y(d):
        return {"tile": z * NY + lax.rem(y + d + NY, NY)}

    partner = {"vintage": 1 - v}

    barrier = pltpu.get_barrier_semaphore()
    peers = [along_z(sg * e) for e in range(1, max(FAR, 1) + 1) for sg in SIGNS]
    peers += [along_y(k) for k in range(1, NY)] + [partner]
    for peer in peers:
        pl.semaphore_signal(barrier, inc=1, device_id=peer, device_id_type=MESH)

    load_obs = pltpu.make_async_copy(observed.at[0, 0], s["obs"], s["local_sem"].at[0])
    load_obs.start()

    started = []

    def send(src, dst, dev):
        i = len(started)
        copy = pltpu.make_async_remote_copy(
            src_ref=src,
            dst_ref=dst,
            send_sem=s["send"].at[i],
            recv_sem=s["recv"].at[i],
            device_id=dev,
            device_id_type=MESH,
        )
        copy.start()
        started.append(copy)
        return copy

    def pick(rel, k, slot, side):
        owner = lax.rem(z + rel + NZ, NZ) * NY + lax.rem(y + k, NY)
        return pairs[v, slot, side, owner]

    commons = (common_left, common_right)
    innovs = (innov_left, innov_right)
    for side in range(2):
        for src, dst in ((commons[side], s["common"][side]), (innovs[side], s["innov"][side])):
            x = src[...].astype(F32)
            dst[pl.ds(0, NB * 8, 2), :] = x[:, :HALF]
            dst[pl.ds(1, NB * 8, 2), :] = x[:, HALF:]
        joined = (s["common"][side][...] + s["innov"][side][...]).astype(BF16)
        s["own"][side][...] = joined.reshape(NB, 16, HALF)

    pl.semaphore_wait(barrier, len(peers))

    dense = {}
    for n in range(2):
        for g, sign in enumerate(SIGNS):
            side = streams(sign)[n]
            dense[g, 1, side] = send(s["own"][side], s["dense"][g][0][side], along_z(sign))

    def choose(bufs, o):
        for k in range(NY):
            for side in range(2):
                for slot in range(2):
                    piece = bufs[side][pick(0, k, slot, side)]
                    if k == 0:
                        s["g"][0, o, side, slot] = piece
                    else:
                        s["ysend"][k - 1, o, side, slot] = piece

    arrivals = []

    def spread(o0, n):
        for k in range(1, NY):
            arrivals.append(
                send(s["ysend"].at[k - 1, pl.ds(o0, n)], s["g"].at[k, pl.ds(o0, n)], along_y(k))
            )

    def build_order():
        row = lax.broadcasted_iota(jnp.int32, (EXT, HALF), 0)
        lane = lax.broadcasted_iota(jnp.int32, (EXT, HALF), 1)
        k, o, j = row >> 7, (row >> 3) & 15, row & 7
        dist = NZ // 2 - ((o + 1) >> 1)
        rel = jnp.where((o & 1) == 1, dist, -dist)
        target = 64 * j + ((z + rel + NZ) & (NZ - 1)) * NY + ((y - k + NY) & (NY - 1))
        for c in range(EXT // HALF):
            s["order"][:, c * HALF : (c + 1) * HALF] = jnp.where(
                target == lane + c * HALF, 1.0, 0.0
            ).astype(BF16)

    def order_tile(slot):
        order = s["order"][...]
        turned = dot(order, s["obs"][slot]).astype(BF16)
        for h in range(2):
            cols = slice(h * EXT, (h + 1) * EXT)
            s["obs_o"][slot, :, cols] = dot(turned[:, cols], order, 1, 1).astype(BF16)

    def order_masks(slot):
        order = s["order"][...]
        rows = jnp.broadcast_to(row_mask[slot : slot + 1, :].astype(F32), (HALF, EXT)).astype(BF16)
        cols = jnp.broadcast_to(col_mask[slot : slot + 1, :].astype(F32), (16, EXT)).astype(BF16)
        by_row = dot(order, rows, 1, 1)
        by_col = dot(cols, order, 1, 1)[0:1, :]
        weight = jnp.concatenate([by_row] * (EXT // HALF), axis=1) * by_col
        s["weight"][slot] = (weight * live[v, slot, t].astype(F32)).astype(BF16)

    def one_hot(rel, side):
        row = lax.broadcasted_iota(jnp.int32, (NB * 16, HALF), 0)
        lane = lax.broadcasted_iota(jnp.int32, (1, HALF), 1)
        target = jnp.zeros((1, HALF), jnp.int32)
        for slot in range(2):
            for k in range(NY):
                target = jnp.where(
                    (lane >> 4) == slot * NY + k, pick(rel, k, slot, side), target
                )
        return jnp.where(row == target * 16 + (lane & 15), 1.0, 0.0).astype(BF16)

    def build_own_hot():
        for side in range(2):
            hot = one_hot(0, side)
            s["hot"][side][...] = hot
            for g in range(2):
                s["hot_far"][g][side][:, :HALF] = hot

    def build_far_hot(g):
        sign = SIGNS[g]
        for side in range(2):
            for e in range(1, far_count(sign, side) + 1):
                s["hot_far"][g][side][:, e * HALF : (e + 1) * HALF] = one_hot(-sign * e, side)

    def first_tile():
        load_obs.wait()
        order_tile(0)

    aside = [
        [build_order, first_tile],
        [lambda: order_tile(1)],
        [lambda: order_masks(0), lambda: order_masks(1)],
        [build_own_hot],
        [lambda: build_far_hot(0), lambda: build_far_hot(1)],
    ]
    aside += [[]] * NEAR

    choose(s["own"], place(0))
    spread(place(0), 1)
    for job in aside[0]:
        job()

    picks = {}
    for h in range(1, NEAR + 1):
        for n in range(2):
            for g, sign in enumerate(SIGNS):
                side = streams(sign)[n]
                dense[g, h, side].wait_recv()
                here = s["dense"][g][h - 1][side]
                if h < NEAR:
                    dense[g, h + 1, side] = send(here, s["dense"][g][h][side], along_z(sign))
                else:
                    for e in range(far_count(sign, side), 0, -1):
                        out = s["far_send"][g][side].at[e - 1]
                        for k in range(NY):
                            for slot in range(2):
                                out[k, slot] = here[pick(sign * e, k, slot, side)]
                        picks[g, e, side] = send(out, s["far"][g][side].at[e - 1], along_z(sign * e))
        for g, sign in enumerate(SIGNS):
            choose(s["dense"][g][h - 1], place(-sign * h))
        spread(place(h), 2)
        for job in aside[h]:
            job()
    for jobs in aside[NEAR + 1 : 5]:
        for job in jobs:
            job()

    for e in range(1, FAR + 1):
        d = NEAR + e
        for g, sign in enumerate(SIGNS):
            for side in range(2):
                if e <= far_count(sign, side):
                    picks[g, e, side].wait_recv()
                    o = place(-sign * d)
                    s["g"][0, o, side] = s["far"][g][side][e - 1, 0]
                    for k in range(1, NY):
                        s["ysend"][k - 1, o, side] = s["far"][g][side][e - 1, k]
        spread(place(d), 1 if d == NZ // 2 else 2)
    for copy in arrivals:
        copy.wait_recv()

    def parts(side, slot):
        x = s["g"][:, :, side, slot].reshape(2 * EXT, HALF).astype(F32)
        s["wide"][side][...] = x
        real = s["wide"][side][pl.ds(0, EXT, 2), :].astype(BF16)
        imag = s["wide"][side][pl.ds(1, EXT, 2), :].astype(BF16)
        return real, imag

    def keep(delta, side, slot):
        s["wide"][side][pl.ds(0, EXT, 2), :] = delta[:, :HALF]
        s["wide"][side][pl.ds(1, EXT, 2), :] = delta[:, HALF:]
        pieces = s["wide"][side][...].astype(BF16).reshape(NY, NZ, 16, HALF)
        s["q"][slot, 0, :, side] = pieces[0]
        for k in range(1, NY):
            s["back"][slot, k - 1, :, side] = pieces[k]

    groups = ((0, 3), (3, 4), (7, 4), (11, 5))
    back = {}
    scale = 1.0 / EXT
    for slot in range(2):
        a_re, a_im = parts(0, slot)
        b_re, b_im = parts(1, slot)
        a = jnp.concatenate([a_re, a_im], axis=1)
        s_re = jnp.concatenate([b_re, -b_im], axis=1)
        s_im = jnp.concatenate([b_im, b_re], axis=1)
        t_re = jnp.concatenate([a_re, -a_im], axis=1)
        t_im = jnp.concatenate([a_im, a_re], axis=1)
        weight = s["weight"][slot].astype(F32)
        m_re = (weight * (dot(a, s_re, 1, 1) - s["obs_o"][slot, :, :EXT].astype(F32))).astype(BF16)
        m_im = (weight * (dot(a, s_im, 1, 1) - s["obs_o"][slot, :, EXT:].astype(F32))).astype(BF16)
        keep((dot(m_re, s_re) + dot(m_im, s_im)) * scale, 0, slot)
        keep((dot(m_re, t_re, 0, 0) + dot(m_im, t_im, 0, 0)) * scale, 1, slot)
        for i, (o0, n) in enumerate(groups):
            for k in range(1, NY):
                back[slot, i, k] = send(
                    s["back"].at[slot, k - 1, pl.ds(o0, n)],
                    s["q"].at[slot, k, pl.ds(o0, n)],
                    along_y(-k),
                )

    def arrived(i):
        for slot in range(2):
            for k in range(1, NY):
                back[slot, i, k].wait_recv()

    def own_picks(rel, side):
        return s["q"][:, :, place(rel), side].reshape(HALF, HALF)

    ready = 0
    raw = {}
    for e in range(FAR, 0, -1):
        d = NEAR + e
        while sum(groups[ready - 1]) * (ready > 0) <= place(-d):
            arrived(ready)
            ready += 1
        for n in range(2):
            for g, sign in enumerate(SIGNS):
                side = streams(sign)[n]
                if e <= far_count(sign, side):
                    rows = pl.ds(e * HALF, HALF)
                    s["raw_send"][g][side][rows, :] = own_picks(sign * d, side)
                    raw[g, e, side] = send(
                        s["raw_send"][g][side].at[rows], s["raw"][g][side].at[rows], along_z(sign * e)
                    )
    chain = {}
    while ready < len(groups):
        arrived(ready)
        ready += 1
    for n in range(2):
        for g, sign in enumerate(SIGNS):
            side = streams(sign)[n]
            s["raw"][g][side][0:HALF, :] = own_picks(sign * NEAR, side)
    for n in range(2):
        for g, sign in enumerate(SIGNS):
            side = streams(sign)[n]
            count = far_count(sign, side)
            for e in range(1, count + 1):
                raw[g, e, side].wait_recv()
            depth = (count + 1) * HALF
            total = dot(s["hot_far"][g][side][:, :depth], s["raw"][g][side][0:depth, :])
            s["sum_send"][g][NEAR - 1][side][...] = total.astype(BF16)
            chain[g, NEAR - 1, side] = send(
                s["sum_send"][g][NEAR - 1][side], s["sum"][g][NEAR - 1][side], along_z(sign)
            )
    for h in range(NEAR - 1, 0, -1):
        for side in range(2):
            both = jnp.concatenate([own_picks(h, side), own_picks(-h, side)], axis=1)
            s["add"][side][...] = dot(s["hot"][side][...], both)
        for n in range(2):
            for g, sign in enumerate(SIGNS):
                side = streams(sign)[n]
                chain[g, h, side].wait_recv()
                total = s["sum"][g][h][side][...].astype(F32)
                total = total + s["add"][side][:, g * HALF : (g + 1) * HALF]
                s["sum_send"][g][h - 1][side][...] = total.astype(BF16)
                chain[g, h - 1, side] = send(
                    s["sum_send"][g][h - 1][side], s["sum"][g][h - 1][side], along_z(sign)
                )
    swap = []
    for side in range(2):
        s["grad"][side][...] = dot(s["hot"][side][...], own_picks(0, side))
    for side in range(2):
        for g in range(2):
            chain[g, 0, side].wait_recv()
        s["grad"][side][...] = (
            s["grad"][side][...]
            + s["sum"][0][0][side][...].astype(F32)
            + s["sum"][1][0][side][...].astype(F32)
        )
        swap.append(send(s["grad"][side], s["other"][side], partner))
    for side, out in enumerate((out_innov_left, out_innov_right)):
        innov = s["innov"][side][...]
        out[...] = innov - step_size * (s["grad"][side][...] + shrink * innov)
    for side, out in enumerate((out_common_left, out_common_right)):
        swap[side].wait_recv()
        out[...] = s["common"][side][...] - step_size * (s["grad"][side][...] + s["other"][side][...])
    for copy in started:
        copy.wait_send()


def shard(dtype=BF16):
    return pltpu.VMEM((NB * 16, HALF), dtype)


def scratch():
    blocks = pltpu.VMEM((NB, 16, HALF), BF16)
    exchange = (NZ, 2, 2, 16, HALF)
    copies = 4 * 2 * NEAR + 4 * (4 * FAR - 2) // 2 + (NEAR + FAR + 1) * 3 + 24 + 2
    far = [
        [pltpu.VMEM((far_count(sign, side), NY, 2, 16, HALF), BF16) for side in range(2)]
        for sign in SIGNS
    ]
    raw = [
        [pltpu.VMEM(((far_count(sign, side) + 1) * HALF, HALF), BF16) for side in range(2)]
        for sign in SIGNS
    ]
    hot_far = [
        [pltpu.VMEM((NB * 16, (far_count(sign, side) + 1) * HALF), BF16) for side in range(2)]
        for sign in SIGNS
    ]
    return {
        "common": [shard(F32)] * 2,
        "innov": [shard(F32)] * 2,
        "grad": [shard(F32)] * 2,
        "other": [shard(F32)] * 2,
        "own": [blocks] * 2,
        "dense": [[[blocks] * 2 for _ in range(NEAR)] for _ in range(2)],
        "far_send": far,
        "far": far,
        "ysend": pltpu.VMEM((NY - 1,) + exchange, BF16),
        "g": pltpu.VMEM((NY,) + exchange, BF16),
        "obs": pltpu.VMEM((2, EXT, 2 * EXT), BF16),
        "obs_o": pltpu.VMEM((2, EXT, 2 * EXT), BF16),
        "order": pltpu.VMEM((EXT, EXT), BF16),
        "weight": pltpu.VMEM((2, EXT, EXT), BF16),
        "hot": [shard()] * 2,
        "hot_far": hot_far,
        "wide": [pltpu.VMEM((2 * EXT, HALF), F32)] * 2,
        "back": pltpu.VMEM((2, NY - 1, NZ, 2, 16, HALF), BF16),
        "q": pltpu.VMEM((2, NY, NZ, 2, 16, HALF), BF16),
        "raw_send": raw,
        "raw": raw,
        "sum_send": [[[shard()] * 2 for _ in range(NEAR)] for _ in range(2)],
        "sum": [[[shard()] * 2 for _ in range(NEAR)] for _ in range(2)],
        "add": [pltpu.VMEM((NB * 16, 2 * HALF), F32)] * 2,
        "send": pltpu.SemaphoreType.DMA((copies,)),
        "recv": pltpu.SemaphoreType.DMA((copies,)),
        "local_sem": pltpu.SemaphoreType.DMA((1,)),
    }


def per_device(
    observed,
    common_left,
    common_right,
    innov_left,
    innov_right,
    tile_block_pairs,
    live,
    row_mask,
    col_mask,
):
    rows, width = common_left.shape[0], common_left.shape[2]
    vmem = pl.BlockSpec(memory_space=pltpu.VMEM)
    smem = pl.BlockSpec(memory_space=pltpu.SMEM)
    outs = pl.pallas_call(
        kernel,
        out_shape=[jax.ShapeDtypeStruct((2 * rows, HALF), F32)] * 4,
        in_specs=[smem, smem, pl.BlockSpec(memory_space=pl.ANY)] + [vmem] * 6,
        out_specs=[vmem] * 4,
        scratch_shapes=[scratch()],
        compiler_params=pltpu.CompilerParams(
            collective_id=0, has_side_effects=True, vmem_limit_bytes=56 * 1024 * 1024
        ),
    )(
        tile_block_pairs.transpose(0, 2, 3, 1),
        live.transpose(0, 2, 1),
        observed,
        common_left.reshape(rows, width),
        common_right.reshape(rows, width),
        innov_left.reshape(rows, width),
        innov_right.reshape(rows, width),
        row_mask.reshape(2, EXT),
        col_mask.reshape(2, EXT),
    )
    return (
        outs[0].reshape(rows, 1, width),
        outs[1].reshape(rows, 1, width),
        outs[2].reshape(1, rows, 1, width),
        outs[3].reshape(1, rows, 1, width),
    )


def solution(mesh):
    placed = (
        P("vintage", "tile", "freq", None, None),
        P("freq", "tile", None),
        P("freq", "tile", None),
        P("vintage", "freq", "tile", None),
        P("vintage", "freq", "tile", None),
        P(None, None, "freq", None),
        P(None, None, "freq"),
        P("vintage", "tile", "freq", None),
        P("vintage", "tile", "freq", None),
    )
    return jax.shard_map(
        per_device,
        mesh=mesh,
        in_specs=placed,
        out_specs=(
            P("freq", "tile", None),
            P("freq", "tile", None),
            P("vintage", "freq", "tile", None),
            P("vintage", "freq", "tile", None),
        ),
        check_vma=False,
    )
```

```python
import jax
import jax.numpy as jnp
from jax import lax
from jax.experimental import pallas as pl
from jax.experimental.pallas import tpu as pltpu
from jax.sharding import PartitionSpec as P

MESH = pl.DeviceIdType.MESH
BF16, F32 = jnp.bfloat16, jnp.float32

step_size = 8.0
shrink = 0.5

NZ, NY = 16, 4
EXT = 512
NB = 32
HALF = 128
NEAR = 3
FAR = NZ // 2 - NEAR
SIGNS = (1, -1)


def place(rel):
    if abs(rel) == NZ // 2:
        return 0
    far = 2 * (NZ // 2 - abs(rel))
    return far - 1 if rel >= 0 else far


def streams(sign):
    return (0, 1) if sign > 0 else (1, 0)


def far_count(sign, side):
    return FAR if streams(sign)[0] == side else FAR - 1


def dot(a, b, ca=1, cb=0):
    return lax.dot_general(a, b, (((ca,), (cb,)), ((), ())), preferred_element_type=F32)


def kernel(
    pairs,
    live,
    observed,
    common_left,
    common_right,
    innov_left,
    innov_right,
    row_mask,
    col_mask,
    out_common_left,
    out_common_right,
    out_innov_left,
    out_innov_right,
    s,
):
    v = lax.axis_index("vintage")
    t = lax.axis_index("tile")
    z, y = t // NY, t % NY

    def along_z(d):
        return {"tile": lax.rem(z + d + NZ, NZ) * NY + y}

    def along_y(d):
        return {"tile": z * NY + lax.rem(y + d + NY, NY)}

    partner = {"vintage": 1 - v}

    barrier = pltpu.get_barrier_semaphore()
    peers = [along_z(sg * e) for e in range(1, max(FAR, 1) + 1) for sg in SIGNS]
    peers += [along_y(k) for k in range(1, NY)] + [partner]
    for peer in peers:
        pl.semaphore_signal(barrier, inc=1, device_id=peer, device_id_type=MESH)

    load_obs = pltpu.make_async_copy(observed.at[0, 0], s["obs"], s["local_sem"].at[0])
    load_obs.start()

    started, gone = [], set()

    def leave(copies):
        for copy in copies:
            copy.wait_send()
            gone.add(id(copy))

    def send(src, dst, dev):
        i = len(started)
        copy = pltpu.make_async_remote_copy(
            src_ref=src,
            dst_ref=dst,
            send_sem=s["send"].at[i],
            recv_sem=s["recv"].at[i],
            device_id=dev,
            device_id_type=MESH,
        )
        copy.start()
        started.append(copy)
        return copy

    def pick(rel, k, slot, side):
        owner = lax.rem(z + rel + NZ, NZ) * NY + lax.rem(y + k, NY)
        return pairs[v, slot, side, owner]

    commons = (common_left, common_right)
    innovs = (innov_left, innov_right)
    for side in range(2):
        for src, dst in ((commons[side], s["common"][side]), (innovs[side], s["innov"][side])):
            x = src[...].astype(F32)
            dst[pl.ds(0, NB * 8, 2), :] = x[:, :HALF]
            dst[pl.ds(1, NB * 8, 2), :] = x[:, HALF:]
        joined = (s["common"][side][...] + s["innov"][side][...]).astype(BF16)
        s["own"][side][...] = joined.reshape(NB, 16, HALF)

    pl.semaphore_wait(barrier, len(peers))

    dense = {}

    def first_hop(n):
        for g, sign in enumerate(SIGNS):
            side = streams(sign)[n]
            dense[g, 1, side] = send(s["own"][side], s["dense"][g][0][side], along_z(sign))

    first_hop(0)

    def choose(bufs, o):
        for k in range(NY):
            for side in range(2):
                for slot in range(2):
                    piece = bufs[side][pick(0, k, slot, side)]
                    if k == 0:
                        s["g"][slot, 0, o, side] = piece
                    else:
                        s["ysend"][slot, k - 1, o, side] = piece

    def spread(slots, o0, n):
        return [
            send(
                s["ysend"].at[slots, k - 1, pl.ds(o0, n)],
                s["g"].at[slots, k, pl.ds(o0, n)],
                along_y(k),
            )
            for k in range(1, NY)
        ]

    both_slots = pl.ds(0, 2)

    def build_order():
        row = lax.broadcasted_iota(jnp.int32, (EXT, HALF), 0)
        lane = lax.broadcasted_iota(jnp.int32, (EXT, HALF), 1)
        k, o, j = row >> 7, (row >> 3) & 15, row & 7
        dist = NZ // 2 - ((o + 1) >> 1)
        rel = jnp.where((o & 1) == 1, dist, -dist)
        target = 64 * j + ((z + rel + NZ) & (NZ - 1)) * NY + ((y - k + NY) & (NY - 1))
        for c in range(EXT // HALF):
            s["order"][:, c * HALF : (c + 1) * HALF] = jnp.where(
                target == lane + c * HALF, 1.0, 0.0
            ).astype(BF16)

    def order_tile(slot):
        order = s["order"][...]
        turned = dot(order, s["obs"][slot]).astype(BF16)
        for h in range(2):
            cols = slice(h * EXT, (h + 1) * EXT)
            s["obs_o"][slot, :, cols] = dot(turned[:, cols], order, 1, 1).astype(BF16)

    def order_masks(slot):
        order = s["order"][...]
        rows = jnp.broadcast_to(row_mask[slot : slot + 1, :].astype(F32), (HALF, EXT)).astype(BF16)
        cols = jnp.broadcast_to(col_mask[slot : slot + 1, :].astype(F32), (16, EXT)).astype(BF16)
        by_row = dot(order, rows, 1, 1)
        by_col = dot(cols, order, 1, 1)[0:1, :]
        weight = jnp.concatenate([by_row] * (EXT // HALF), axis=1) * by_col
        s["weight"][slot] = (weight * live[v, slot, t].astype(F32)).astype(BF16)

    def one_hot(rel, side):
        row = lax.broadcasted_iota(jnp.int32, (NB * 16, HALF), 0)
        lane = lax.broadcasted_iota(jnp.int32, (1, HALF), 1)
        target = jnp.zeros((1, HALF), jnp.int32)
        for slot in range(2):
            for k in range(NY):
                target = jnp.where(
                    (lane >> 4) == slot * NY + k, pick(rel, k, slot, side), target
                )
        return jnp.where(row == target * 16 + (lane & 15), 1.0, 0.0).astype(BF16)

    def build_own_hot():
        for side in range(2):
            hot = one_hot(0, side)
            s["hot"][side][...] = hot
            for g in range(2):
                s["hot_far"][g][side][:, :HALF] = hot

    def build_far_hot(g):
        sign = SIGNS[g]
        for side in range(2):
            for e in range(1, far_count(sign, side) + 1):
                s["hot_far"][g][side][:, e * HALF : (e + 1) * HALF] = one_hot(-sign * e, side)

    def first_tile():
        load_obs.wait()
        order_tile(0)

    aside = [
        [lambda: order_tile(1)],
        [lambda: order_masks(0), lambda: order_masks(1)],
        [build_own_hot, lambda: build_far_hot(0)],
        [lambda: build_far_hot(1)],
    ]

    choose(s["own"], place(0))
    near = spread(both_slots, place(0), 1)
    build_order()
    leave([dense[g, 1, streams(sign)[0]] for g, sign in enumerate(SIGNS)])
    first_hop(1)
    first_tile()

    picks = {}

    def pick_far(g, side, slot):
        sign = SIGNS[g]
        here = s["dense"][g][NEAR - 1][side]
        for e in range(far_count(sign, side), 0, -1):
            out = s["far_send"][g][side].at[slot, e - 1]
            for k in range(NY):
                out[k] = here[pick(sign * e, k, slot, side)]
            picks[g, e, side, slot] = send(
                out, s["far"][g][side].at[slot, e - 1], along_z(sign * e)
            )

    for h in range(1, NEAR + 1):
        for n in range(2):
            for g, sign in enumerate(SIGNS):
                side = streams(sign)[n]
                dense[g, h, side].wait_recv()
                if h < NEAR:
                    dense[g, h + 1, side] = send(
                        s["dense"][g][h - 1][side], s["dense"][g][h][side], along_z(sign)
                    )
                else:
                    pick_far(g, side, 0)
            if n == 0 and h < NEAR and aside:
                for job in aside.pop(0):
                    job()
        for g, sign in enumerate(SIGNS):
            choose(s["dense"][g][h - 1], place(-sign * h))
        near += spread(both_slots, place(h), 2)
    for jobs in aside:
        for job in jobs:
            job()
    leave([picks[key] for key in picks if key[3] == 0])
    for n in range(2):
        for g, sign in enumerate(SIGNS):
            pick_far(g, streams(sign)[n], 1)

    def far_in(slot):
        copies = []
        for e in range(FAR, 0, -1):
            d = NEAR + e
            for g, sign in enumerate(SIGNS):
                for side in range(2):
                    if e <= far_count(sign, side):
                        picks[g, e, side, slot].wait_recv()
                        o = place(-sign * d)
                        s["g"][slot, 0, o, side] = s["far"][g][side][slot, e - 1, 0]
                        for k in range(1, NY):
                            s["ysend"][slot, k - 1, o, side] = s["far"][g][side][slot, e - 1, k]
            copies += spread(slot, place(d), 1 if d == NZ // 2 else 2)
        return copies

    def parts(side, slot):
        x = s["g"][slot, :, :, side].reshape(2 * EXT, HALF).astype(F32)
        s["wide"][side][...] = x
        real = s["wide"][side][pl.ds(0, EXT, 2), :].astype(BF16)
        imag = s["wide"][side][pl.ds(1, EXT, 2), :].astype(BF16)
        return real, imag

    def keep(delta, side, slot):
        s["wide"][side][pl.ds(0, EXT, 2), :] = delta[:, :HALF]
        s["wide"][side][pl.ds(1, EXT, 2), :] = delta[:, HALF:]
        pieces = s["wide"][side][...].astype(BF16).reshape(NY, NZ, 16, HALF)
        s["q"][slot, 0, :, side] = pieces[0]
        for k in range(1, NY):
            s["back"][slot, k - 1, :, side] = pieces[k]

    groups = ((0, 3), (3, 2 * FAR - 4), (2 * FAR - 1, 4), (2 * FAR + 3, 2 * NEAR - 3))
    back = {}
    scale = 1.0 / EXT

    def tile(slot):
        a_re, a_im = parts(0, slot)
        b_re, b_im = parts(1, slot)
        a = jnp.concatenate([a_re, a_im], axis=1)
        s_re = jnp.concatenate([b_re, -b_im], axis=1)
        s_im = jnp.concatenate([b_im, b_re], axis=1)
        t_re = jnp.concatenate([a_re, -a_im], axis=1)
        t_im = jnp.concatenate([a_im, a_re], axis=1)
        weight = s["weight"][slot].astype(F32)
        m_re = (weight * (dot(a, s_re, 1, 1) - s["obs_o"][slot, :, :EXT].astype(F32))).astype(BF16)
        m_im = (weight * (dot(a, s_im, 1, 1) - s["obs_o"][slot, :, EXT:].astype(F32))).astype(BF16)
        keep((dot(m_re, s_re) + dot(m_im, s_im)) * scale, 0, slot)
        keep((dot(m_re, t_re, 0, 0) + dot(m_im, t_im, 0, 0)) * scale, 1, slot)
        for i, (o0, n) in enumerate(groups):
            for k in range(1, NY):
                back[slot, i, k] = send(
                    s["back"].at[slot, k - 1, pl.ds(o0, n)],
                    s["q"].at[slot, k, pl.ds(o0, n)],
                    along_y(-k),
                )

    def arrived(slot, i):
        for k in range(1, NY):
            back[slot, i, k].wait_recv()

    def own_picks(rel, side):
        return s["q"][:, :, place(rel), side].reshape(HALF, HALF)

    raw = {}

    def far_out(slot):
        arrived(slot, 0)
        arrived(slot, 1)
        for n in range(2):
            for g, sign in enumerate(SIGNS):
                side = streams(sign)[n]
                for e in range(far_count(sign, side), 0, -1):
                    rows = pl.ds(e * HALF + slot * (HALF // 2), HALF // 2)
                    mine = s["q"][slot, :, place(sign * (NEAR + e)), side]
                    s["raw_send"][g][side][rows, :] = mine.reshape(HALF // 2, HALF)
                    raw[g, e, side, slot] = send(
                        s["raw_send"][g][side].at[rows], s["raw"][g][side].at[rows], along_z(sign * e)
                    )

    early = far_in(0)
    for copy in near + early:
        copy.wait_recv()
    tile(0)
    late = far_in(1)
    far_out(0)
    for copy in late:
        copy.wait_recv()
    tile(1)
    far_out(1)
    for slot in range(2):
        arrived(slot, 2)
    for g, sign in enumerate(SIGNS):
        for side in range(2):
            s["raw"][g][side][0:HALF, :] = own_picks(sign * NEAR, side)

    def own_sums(h):
        for side in range(2):
            both = jnp.concatenate([own_picks(h, side), own_picks(-h, side)], axis=1)
            s["add"][h - 1][side][...] = dot(s["hot"][side][...], both)

    own_sums(NEAR - 1)
    chain = {}
    for n in range(2):
        for g, sign in enumerate(SIGNS):
            side = streams(sign)[n]
            count = far_count(sign, side)
            for e in range(count, 0, -1):
                for slot in range(2):
                    raw[g, e, side, slot].wait_recv()
            depth = (count + 1) * HALF
            total = dot(s["hot_far"][g][side][:, :depth], s["raw"][g][side][0:depth, :])
            s["sum_send"][g][NEAR - 1][side][...] = total.astype(BF16)
            if n == 1:
                leave([chain[g, NEAR - 1, streams(sign)[0]]])
            chain[g, NEAR - 1, side] = send(
                s["sum_send"][g][NEAR - 1][side], s["sum"][g][NEAR - 1][side], along_z(sign)
            )
    for slot in range(2):
        arrived(slot, 3)
    for h in range(NEAR - 2, 0, -1):
        own_sums(h)
    for side in range(2):
        s["grad"][side][...] = dot(s["hot"][side][...], own_picks(0, side))
    for h in range(NEAR - 1, 0, -1):
        for n in range(2):
            for g, sign in enumerate(SIGNS):
                side = streams(sign)[n]
                chain[g, h, side].wait_recv()
                total = s["sum"][g][h][side][...].astype(F32)
                total = total + s["add"][h - 1][side][:, g * HALF : (g + 1) * HALF]
                s["sum_send"][g][h - 1][side][...] = total.astype(BF16)
                chain[g, h - 1, side] = send(
                    s["sum_send"][g][h - 1][side], s["sum"][g][h - 1][side], along_z(sign)
                )
    swap = []
    for side in range(2):
        for g in range(2):
            chain[g, 0, side].wait_recv()
        s["grad"][side][...] = (
            s["grad"][side][...]
            + s["sum"][0][0][side][...].astype(F32)
            + s["sum"][1][0][side][...].astype(F32)
        )
        swap.append(send(s["grad"][side], s["other"][side], partner))
    for side, out in enumerate((out_innov_left, out_innov_right)):
        innov = s["innov"][side][...]
        out[...] = innov - step_size * (s["grad"][side][...] + shrink * innov)
    for side, out in enumerate((out_common_left, out_common_right)):
        swap[side].wait_recv()
        out[...] = s["common"][side][...] - step_size * (s["grad"][side][...] + s["other"][side][...])
    leave([copy for copy in started if id(copy) not in gone])


def hand_over(*refs):
    given, outs, held, sems = refs[:4], refs[4:8], refs[8], refs[9]
    inward = [pltpu.make_async_copy(given[i], held.at[i], sems.at[i]) for i in range(4)]
    outward = [pltpu.make_async_copy(held.at[i], outs[i], sems.at[4 + i]) for i in range(4)]
    for copy in inward:
        copy.start()
    for i in range(4):
        inward[i].wait()
        outward[i].start()
    for copy in outward:
        copy.wait()


def shard(dtype=BF16):
    return pltpu.VMEM((NB * 16, HALF), dtype)


def scratch():
    blocks = pltpu.VMEM((NB, 16, HALF), BF16)
    exchange = (NZ, 2, 16, HALF)
    copies = 8 * NEAR + 4 * (4 * FAR - 2) + (NEAR + 2 * FAR + 1) * 3 + 24 + 2
    far = [
        [pltpu.VMEM((2, far_count(sign, side), NY, 16, HALF), BF16) for side in range(2)]
        for sign in SIGNS
    ]
    raw = [
        [pltpu.VMEM(((far_count(sign, side) + 1) * HALF, HALF), BF16) for side in range(2)]
        for sign in SIGNS
    ]
    hot_far = [
        [pltpu.VMEM((NB * 16, (far_count(sign, side) + 1) * HALF), BF16) for side in range(2)]
        for sign in SIGNS
    ]
    return {
        "common": [shard(F32)] * 2,
        "innov": [shard(F32)] * 2,
        "grad": [shard(F32)] * 2,
        "other": [shard(F32)] * 2,
        "own": [blocks] * 2,
        "dense": [[[blocks] * 2 for _ in range(NEAR)] for _ in range(2)],
        "far_send": far,
        "far": far,
        "ysend": pltpu.VMEM((2, NY - 1) + exchange, BF16),
        "g": pltpu.VMEM((2, NY) + exchange, BF16),
        "obs": pltpu.VMEM((2, EXT, 2 * EXT), BF16),
        "obs_o": pltpu.VMEM((2, EXT, 2 * EXT), BF16),
        "order": pltpu.VMEM((EXT, EXT), BF16),
        "weight": pltpu.VMEM((2, EXT, EXT), BF16),
        "hot": [shard()] * 2,
        "hot_far": hot_far,
        "wide": [pltpu.VMEM((2 * EXT, HALF), F32)] * 2,
        "back": pltpu.VMEM((2, NY - 1) + exchange, BF16),
        "q": pltpu.VMEM((2, NY) + exchange, BF16),
        "raw_send": raw,
        "raw": raw,
        "sum_send": [[[shard()] * 2 for _ in range(NEAR)] for _ in range(2)],
        "sum": [[[shard()] * 2 for _ in range(NEAR)] for _ in range(2)],
        "add": [[pltpu.VMEM((NB * 16, 2 * HALF), F32)] * 2 for _ in range(NEAR - 1)],
        "send": pltpu.SemaphoreType.DMA((copies,)),
        "recv": pltpu.SemaphoreType.DMA((copies,)),
        "local_sem": pltpu.SemaphoreType.DMA((1,)),
    }


def per_device(
    observed,
    common_left,
    common_right,
    innov_left,
    innov_right,
    tile_block_pairs,
    live,
    row_mask,
    col_mask,
):
    rows, width = common_left.shape[0], common_left.shape[2]
    vmem = pl.BlockSpec(memory_space=pltpu.VMEM)
    smem = pl.BlockSpec(memory_space=pltpu.SMEM)
    outs = pl.pallas_call(
        kernel,
        out_shape=[jax.ShapeDtypeStruct((2 * rows, HALF), F32)] * 4,
        in_specs=[smem, smem, pl.BlockSpec(memory_space=pl.ANY)] + [vmem] * 6,
        out_specs=[vmem] * 4,
        scratch_shapes=[scratch()],
        compiler_params=pltpu.CompilerParams(
            collective_id=0, has_side_effects=True, vmem_limit_bytes=56 * 1024 * 1024
        ),
    )(
        tile_block_pairs.transpose(0, 2, 3, 1),
        live.transpose(0, 2, 1),
        observed,
        common_left.reshape(rows, width),
        common_right.reshape(rows, width),
        innov_left.reshape(rows, width),
        innov_right.reshape(rows, width),
        row_mask.reshape(2, EXT),
        col_mask.reshape(2, EXT),
    )
    outs = pl.pallas_call(
        hand_over,
        out_shape=[jax.ShapeDtypeStruct((2 * rows, HALF), F32)] * 4,
        in_specs=[pl.BlockSpec(memory_space=pl.ANY)] * 4,
        out_specs=[pl.BlockSpec(memory_space=pl.ANY)] * 4,
        scratch_shapes=[pltpu.VMEM((4, 2 * rows, HALF), F32), pltpu.SemaphoreType.DMA((8,))],
        compiler_params=pltpu.CompilerParams(vmem_limit_bytes=56 * 1024 * 1024),
    )(*outs)
    return (
        outs[0].reshape(rows, 1, width),
        outs[1].reshape(rows, 1, width),
        outs[2].reshape(1, rows, 1, width),
        outs[3].reshape(1, rows, 1, width),
    )


def solution(mesh):
    placed = (
        P("vintage", "tile", "freq", None, None),
        P("freq", "tile", None),
        P("freq", "tile", None),
        P("vintage", "freq", "tile", None),
        P("vintage", "freq", "tile", None),
        P(None, None, "freq", None),
        P(None, None, "freq"),
        P("vintage", "tile", "freq", None),
        P("vintage", "tile", "freq", None),
    )
    return jax.shard_map(
        per_device,
        mesh=mesh,
        in_specs=placed,
        out_specs=(
            P("freq", "tile", None),
            P("freq", "tile", None),
            P("vintage", "freq", "tile", None),
            P("vintage", "freq", "tile", None),
        ),
        check_vma=False,
    )
```

```python
import jax
import jax.numpy as jnp
from jax import lax
from jax.experimental import pallas as pl
from jax.experimental.pallas import tpu as pltpu
from jax.sharding import PartitionSpec as P

MESH = pl.DeviceIdType.MESH
BF16, F32 = jnp.bfloat16, jnp.float32

step_size = 8.0
shrink = 0.5

NZ, NY = 16, 4
EXT = 512
NB = 32
HALF = 128
NEAR = 3
FAR = NZ // 2 - NEAR
SIGNS = (1, -1)
HALVES = (pl.ds(0, NB // 2), pl.ds(NB // 2, NB // 2))
ROWS = (pl.ds(0, NB * 8), pl.ds(NB * 8, NB * 8))


def place(rel):
    if abs(rel) == NZ // 2:
        return 0
    far = 2 * (NZ // 2 - abs(rel))
    return far - 1 if rel >= 0 else far


def streams(sign):
    return (0, 1) if sign > 0 else (1, 0)


def far_count(sign, side):
    return FAR if streams(sign)[0] == side else FAR - 1


def dot(a, b, ca=1, cb=0):
    return lax.dot_general(a, b, (((ca,), (cb,)), ((), ())), preferred_element_type=F32)


def kernel(
    pairs,
    live,
    observed,
    common_left,
    common_right,
    innov_left,
    innov_right,
    row_mask,
    col_mask,
    out_common_left,
    out_common_right,
    out_innov_left,
    out_innov_right,
    s,
):
    v = lax.axis_index("vintage")
    t = lax.axis_index("tile")
    z, y = t // NY, t % NY

    def along_z(d):
        return {"tile": lax.rem(z + d + NZ, NZ) * NY + y}

    def along_y(d):
        return {"tile": z * NY + lax.rem(y + d + NY, NY)}

    partner = {"vintage": 1 - v}

    barrier = pltpu.get_barrier_semaphore()
    peers = [along_z(sg * e) for e in range(1, max(FAR, 1) + 1) for sg in SIGNS]
    peers += [along_y(k) for k in range(1, NY)] + [partner]
    for peer in peers:
        pl.semaphore_signal(barrier, inc=1, device_id=peer, device_id_type=MESH)

    load_obs = pltpu.make_async_copy(observed.at[0, 0], s["obs"], s["local_sem"].at[0])
    load_obs.start()

    started, gone = [], set()

    def leave(copies):
        for copy in copies:
            copy.wait_send()
            gone.add(id(copy))

    def send(src, dst, dev):
        i = len(started)
        copy = pltpu.make_async_remote_copy(
            src_ref=src,
            dst_ref=dst,
            send_sem=s["send"].at[i],
            recv_sem=s["recv"].at[i],
            device_id=dev,
            device_id_type=MESH,
        )
        copy.start()
        started.append(copy)
        return copy

    def pick(rel, k, slot, side):
        owner = lax.rem(z + rel + NZ, NZ) * NY + lax.rem(y + k, NY)
        return pairs[v, slot, side, owner]

    commons = (common_left, common_right)
    innovs = (innov_left, innov_right)
    for side in range(2):
        for src, dst in ((commons[side], s["common"][side]), (innovs[side], s["innov"][side])):
            x = src[...].astype(F32)
            dst[pl.ds(0, NB * 8, 2), :] = x[:, :HALF]
            dst[pl.ds(1, NB * 8, 2), :] = x[:, HALF:]
        joined = (s["common"][side][...] + s["innov"][side][...]).astype(BF16)
        s["own"][side][...] = joined.reshape(NB, 16, HALF)

    pl.semaphore_wait(barrier, len(peers))

    dense = {}

    def first_hop(n):
        for g, sign in enumerate(SIGNS):
            side = streams(sign)[n]
            for c, blocks in enumerate(HALVES):
                dense[g, 1, side, c] = send(
                    s["own"][side].at[blocks], s["dense"][g][0][side].at[blocks], along_z(sign)
                )

    first_hop(0)

    def choose(bufs, o):
        for k in range(NY):
            for side in range(2):
                for slot in range(2):
                    piece = bufs[side][pick(0, k, slot, side)]
                    if k == 0:
                        s["g"][slot, 0, o, side] = piece
                    else:
                        s["ysend"][slot, k - 1, o, side] = piece

    def spread(slots, o0, n):
        return [
            send(
                s["ysend"].at[slots, k - 1, pl.ds(o0, n)],
                s["g"].at[slots, k, pl.ds(o0, n)],
                along_y(k),
            )
            for k in range(1, NY)
        ]

    both_slots = pl.ds(0, 2)

    def build_order():
        row = lax.broadcasted_iota(jnp.int32, (EXT, HALF), 0)
        lane = lax.broadcasted_iota(jnp.int32, (EXT, HALF), 1)
        k, o, j = row >> 7, (row >> 3) & 15, row & 7
        dist = NZ // 2 - ((o + 1) >> 1)
        rel = jnp.where((o & 1) == 1, dist, -dist)
        target = 64 * j + ((z + rel + NZ) & (NZ - 1)) * NY + ((y - k + NY) & (NY - 1))
        for c in range(EXT // HALF):
            s["order"][:, c * HALF : (c + 1) * HALF] = jnp.where(
                target == lane + c * HALF, 1.0, 0.0
            ).astype(BF16)

    def order_tile(slot):
        order = s["order"][...]
        turned = dot(order, s["obs"][slot]).astype(BF16)
        for h in range(2):
            cols = slice(h * EXT, (h + 1) * EXT)
            s["obs_o"][slot, :, cols] = dot(turned[:, cols], order, 1, 1).astype(BF16)

    def order_masks(slot):
        order = s["order"][...]
        rows = jnp.broadcast_to(row_mask[slot : slot + 1, :].astype(F32), (HALF, EXT)).astype(BF16)
        cols = jnp.broadcast_to(col_mask[slot : slot + 1, :].astype(F32), (16, EXT)).astype(BF16)
        by_row = dot(order, rows, 1, 1)
        by_col = dot(cols, order, 1, 1)[0:1, :]
        weight = jnp.concatenate([by_row] * (EXT // HALF), axis=1) * by_col
        s["weight"][slot] = (weight * live[v, slot, t].astype(F32)).astype(BF16)

    def one_hot(rel, side):
        row = lax.broadcasted_iota(jnp.int32, (NB * 16, HALF), 0)
        lane = lax.broadcasted_iota(jnp.int32, (1, HALF), 1)
        target = jnp.zeros((1, HALF), jnp.int32)
        for slot in range(2):
            for k in range(NY):
                target = jnp.where(
                    (lane >> 4) == slot * NY + k, pick(rel, k, slot, side), target
                )
        return jnp.where(row == target * 16 + (lane & 15), 1.0, 0.0).astype(BF16)

    def build_own_hot():
        for side in range(2):
            hot = one_hot(0, side)
            s["hot"][side][...] = hot
            for g in range(2):
                s["hot_far"][g][side][:, :HALF] = hot

    def build_far_hot(g):
        sign = SIGNS[g]
        for side in range(2):
            for e in range(1, far_count(sign, side) + 1):
                s["hot_far"][g][side][:, e * HALF : (e + 1) * HALF] = one_hot(-sign * e, side)

    choose(s["own"], place(0))
    near = spread(both_slots, place(0), 1)
    build_order()
    leave([dense[g, 1, streams(sign)[0], c] for c in range(2) for g, sign in enumerate(SIGNS)])
    first_hop(1)

    picks = {}

    def pick_far(g, side, slot):
        sign = SIGNS[g]
        here = s["dense"][g][NEAR - 1][side]
        for e in range(far_count(sign, side), 0, -1):
            out = s["far_send"][g][side].at[slot, e - 1]
            for k in range(NY):
                out[k] = here[pick(sign * e, k, slot, side)]
            picks[g, e, side, slot] = send(
                out, s["far"][g][side].at[slot, e - 1], along_z(sign * e)
            )

    for h in range(1, NEAR + 1):
        for n in range(2):
            for c, blocks in enumerate(HALVES):
                for g, sign in enumerate(SIGNS):
                    side = streams(sign)[n]
                    dense[g, h, side, c].wait_recv()
                    if h < NEAR:
                        dense[g, h + 1, side, c] = send(
                            s["dense"][g][h - 1][side].at[blocks],
                            s["dense"][g][h][side].at[blocks],
                            along_z(sign),
                        )
            if h == NEAR:
                for g, sign in enumerate(SIGNS):
                    pick_far(g, streams(sign)[n], 0)
        for g, sign in enumerate(SIGNS):
            choose(s["dense"][g][h - 1], place(-sign * h))
        near += spread(both_slots, place(h), 2)
    load_obs.wait()
    order_tile(0)
    order_masks(0)
    leave([picks[key] for key in picks if key[3] == 0])
    for n in range(2):
        for g, sign in enumerate(SIGNS):
            pick_far(g, streams(sign)[n], 1)
    order_tile(1)
    order_masks(1)

    def far_in(slot):
        copies = []
        for e in range(FAR, 0, -1):
            d = NEAR + e
            for g, sign in enumerate(SIGNS):
                for side in range(2):
                    if e <= far_count(sign, side):
                        picks[g, e, side, slot].wait_recv()
                        o = place(-sign * d)
                        s["g"][slot, 0, o, side] = s["far"][g][side][slot, e - 1, 0]
                        for k in range(1, NY):
                            s["ysend"][slot, k - 1, o, side] = s["far"][g][side][slot, e - 1, k]
            copies += spread(slot, place(d), 1 if d == NZ // 2 else 2)
        return copies

    def parts(side, slot):
        x = s["g"][slot, :, :, side].reshape(2 * EXT, HALF).astype(F32)
        s["wide"][side][...] = x
        real = s["wide"][side][pl.ds(0, EXT, 2), :].astype(BF16)
        imag = s["wide"][side][pl.ds(1, EXT, 2), :].astype(BF16)
        return real, imag

    def keep(delta, side, slot):
        s["wide"][side][pl.ds(0, EXT, 2), :] = delta[:, :HALF]
        s["wide"][side][pl.ds(1, EXT, 2), :] = delta[:, HALF:]
        pieces = s["wide"][side][...].astype(BF16).reshape(NY, NZ, 16, HALF)
        s["q"][slot, 0, :, side] = pieces[0]
        for k in range(1, NY):
            s["back"][slot, k - 1, :, side] = pieces[k]

    groups = ((0, 3), (3, 2 * FAR - 4), (2 * FAR - 1, 4), (2 * FAR + 3, 2 * NEAR - 3))
    back = {}
    scale = 1.0 / EXT

    def tile(slot):
        a_re, a_im = parts(0, slot)
        b_re, b_im = parts(1, slot)
        a = jnp.concatenate([a_re, a_im], axis=1)
        s_re = jnp.concatenate([b_re, -b_im], axis=1)
        s_im = jnp.concatenate([b_im, b_re], axis=1)
        t_re = jnp.concatenate([a_re, -a_im], axis=1)
        t_im = jnp.concatenate([a_im, a_re], axis=1)
        weight = s["weight"][slot].astype(F32)
        m_re = (weight * (dot(a, s_re, 1, 1) - s["obs_o"][slot, :, :EXT].astype(F32))).astype(BF16)
        m_im = (weight * (dot(a, s_im, 1, 1) - s["obs_o"][slot, :, EXT:].astype(F32))).astype(BF16)
        keep((dot(m_re, s_re) + dot(m_im, s_im)) * scale, 0, slot)
        keep((dot(m_re, t_re, 0, 0) + dot(m_im, t_im, 0, 0)) * scale, 1, slot)
        for i, (o0, n) in enumerate(groups):
            for k in range(1, NY):
                back[slot, i, k] = send(
                    s["back"].at[slot, k - 1, pl.ds(o0, n)],
                    s["q"].at[slot, k, pl.ds(o0, n)],
                    along_y(-k),
                )

    def arrived(slot, i):
        for k in range(1, NY):
            back[slot, i, k].wait_recv()

    def own_picks(rel, side):
        return s["q"][:, :, place(rel), side].reshape(HALF, HALF)

    raw = {}

    def far_out(slot):
        arrived(slot, 0)
        arrived(slot, 1)
        for n in range(2):
            for g, sign in enumerate(SIGNS):
                side = streams(sign)[n]
                for e in range(far_count(sign, side), 0, -1):
                    rows = pl.ds(e * HALF + slot * (HALF // 2), HALF // 2)
                    mine = s["q"][slot, :, place(sign * (NEAR + e)), side]
                    s["raw_send"][g][side][rows, :] = mine.reshape(HALF // 2, HALF)
                    raw[g, e, side, slot] = send(
                        s["raw_send"][g][side].at[rows], s["raw"][g][side].at[rows], along_z(sign * e)
                    )

    early = far_in(0)
    for copy in near + early:
        copy.wait_recv()
    tile(0)
    build_own_hot()
    late = far_in(1)
    far_out(0)
    for copy in late:
        copy.wait_recv()
    tile(1)
    far_out(1)
    for g in range(2):
        build_far_hot(g)
    for slot in range(2):
        arrived(slot, 2)
    for g, sign in enumerate(SIGNS):
        for side in range(2):
            s["raw"][g][side][0:HALF, :] = own_picks(sign * NEAR, side)

    def own_sums(h):
        for side in range(2):
            both = jnp.concatenate([own_picks(h, side), own_picks(-h, side)], axis=1)
            s["add"][h - 1][side][...] = dot(s["hot"][side][...], both)

    own_sums(NEAR - 1)
    chain = {}

    def pass_on(g, h, side, c):
        chain[g, h, side, c] = send(
            s["sum_send"][g][h][side].at[ROWS[c]], s["sum"][g][h][side].at[ROWS[c]], along_z(SIGNS[g])
        )

    for n in range(2):
        for g, sign in enumerate(SIGNS):
            side = streams(sign)[n]
            count = far_count(sign, side)
            for e in range(count, 0, -1):
                for slot in range(2):
                    raw[g, e, side, slot].wait_recv()
        for c, rows in enumerate(ROWS):
            for g, sign in enumerate(SIGNS):
                side = streams(sign)[n]
                depth = (far_count(sign, side) + 1) * HALF
                total = dot(s["hot_far"][g][side][rows, :depth], s["raw"][g][side][0:depth, :])
                s["sum_send"][g][NEAR - 1][side][rows, :] = total.astype(BF16)
                if n == 1:
                    leave([chain[g, NEAR - 1, streams(sign)[0], c]])
                pass_on(g, NEAR - 1, side, c)
    for slot in range(2):
        arrived(slot, 3)
    for h in range(NEAR - 2, 0, -1):
        own_sums(h)
    for side in range(2):
        s["grad"][side][...] = dot(s["hot"][side][...], own_picks(0, side))
    for h in range(NEAR - 1, 0, -1):
        for n in range(2):
            for c, rows in enumerate(ROWS):
                for g, sign in enumerate(SIGNS):
                    side = streams(sign)[n]
                    chain[g, h, side, c].wait_recv()
                    total = s["sum"][g][h][side][rows, :].astype(F32)
                    total = total + s["add"][h - 1][side][rows, g * HALF : (g + 1) * HALF]
                    s["sum_send"][g][h - 1][side][rows, :] = total.astype(BF16)
                    pass_on(g, h - 1, side, c)
    swap = {}
    for c, rows in enumerate(ROWS):
        for side in range(2):
            for g in range(2):
                chain[g, 0, side, c].wait_recv()
            s["grad"][side][rows, :] = (
                s["grad"][side][rows, :]
                + s["sum"][0][0][side][rows, :].astype(F32)
                + s["sum"][1][0][side][rows, :].astype(F32)
            )
            swap[side, c] = send(s["grad"][side].at[rows], s["other"][side].at[rows], partner)
    for side, out in enumerate((out_innov_left, out_innov_right)):
        innov = s["innov"][side][...]
        out[...] = innov - step_size * (s["grad"][side][...] + shrink * innov)
    for c, rows in enumerate(ROWS):
        for side, out in enumerate((out_common_left, out_common_right)):
            swap[side, c].wait_recv()
            out[rows, :] = s["common"][side][rows, :] - step_size * (
                s["grad"][side][rows, :] + s["other"][side][rows, :]
            )
    leave([copy for copy in started if id(copy) not in gone])


def hand_over(*refs):
    given, outs, held, sems = refs[:4], refs[4:8], refs[8], refs[9]
    inward = [pltpu.make_async_copy(given[i], held.at[i], sems.at[i]) for i in range(4)]
    outward = [pltpu.make_async_copy(held.at[i], outs[i], sems.at[4 + i]) for i in range(4)]
    for copy in inward:
        copy.start()
    for i in range(4):
        inward[i].wait()
        outward[i].start()
    for copy in outward:
        copy.wait()


def shard(dtype=BF16):
    return pltpu.VMEM((NB * 16, HALF), dtype)


def scratch():
    blocks = pltpu.VMEM((NB, 16, HALF), BF16)
    exchange = (NZ, 2, 16, HALF)
    copies = 16 * NEAR + 4 * (4 * FAR - 2) + (NEAR + 2 * FAR + 1) * 3 + 24 + 4
    far = [
        [pltpu.VMEM((2, far_count(sign, side), NY, 16, HALF), BF16) for side in range(2)]
        for sign in SIGNS
    ]
    raw = [
        [pltpu.VMEM(((far_count(sign, side) + 1) * HALF, HALF), BF16) for side in range(2)]
        for sign in SIGNS
    ]
    hot_far = [
        [pltpu.VMEM((NB * 16, (far_count(sign, side) + 1) * HALF), BF16) for side in range(2)]
        for sign in SIGNS
    ]
    return {
        "common": [shard(F32)] * 2,
        "innov": [shard(F32)] * 2,
        "grad": [shard(F32)] * 2,
        "other": [shard(F32)] * 2,
        "own": [blocks] * 2,
        "dense": [[[blocks] * 2 for _ in range(NEAR)] for _ in range(2)],
        "far_send": far,
        "far": far,
        "ysend": pltpu.VMEM((2, NY - 1) + exchange, BF16),
        "g": pltpu.VMEM((2, NY) + exchange, BF16),
        "obs": pltpu.VMEM((2, EXT, 2 * EXT), BF16),
        "obs_o": pltpu.VMEM((2, EXT, 2 * EXT), BF16),
        "order": pltpu.VMEM((EXT, EXT), BF16),
        "weight": pltpu.VMEM((2, EXT, EXT), BF16),
        "hot": [shard()] * 2,
        "hot_far": hot_far,
        "wide": [pltpu.VMEM((2 * EXT, HALF), F32)] * 2,
        "back": pltpu.VMEM((2, NY - 1) + exchange, BF16),
        "q": pltpu.VMEM((2, NY) + exchange, BF16),
        "raw_send": raw,
        "raw": raw,
        "sum_send": [[[shard()] * 2 for _ in range(NEAR)] for _ in range(2)],
        "sum": [[[shard()] * 2 for _ in range(NEAR)] for _ in range(2)],
        "add": [[pltpu.VMEM((NB * 16, 2 * HALF), F32)] * 2 for _ in range(NEAR - 1)],
        "send": pltpu.SemaphoreType.DMA((copies,)),
        "recv": pltpu.SemaphoreType.DMA((copies,)),
        "local_sem": pltpu.SemaphoreType.DMA((1,)),
    }


def per_device(
    observed,
    common_left,
    common_right,
    innov_left,
    innov_right,
    tile_block_pairs,
    live,
    row_mask,
    col_mask,
):
    rows, width = common_left.shape[0], common_left.shape[2]
    vmem = pl.BlockSpec(memory_space=pltpu.VMEM)
    smem = pl.BlockSpec(memory_space=pltpu.SMEM)
    outs = pl.pallas_call(
        kernel,
        out_shape=[jax.ShapeDtypeStruct((2 * rows, HALF), F32)] * 4,
        in_specs=[smem, smem, pl.BlockSpec(memory_space=pl.ANY)] + [vmem] * 6,
        out_specs=[vmem] * 4,
        scratch_shapes=[scratch()],
        compiler_params=pltpu.CompilerParams(
            collective_id=0, has_side_effects=True, vmem_limit_bytes=56 * 1024 * 1024
        ),
    )(
        tile_block_pairs.transpose(0, 2, 3, 1),
        live.transpose(0, 2, 1),
        observed,
        common_left.reshape(rows, width),
        common_right.reshape(rows, width),
        innov_left.reshape(rows, width),
        innov_right.reshape(rows, width),
        row_mask.reshape(2, EXT),
        col_mask.reshape(2, EXT),
    )
    outs = pl.pallas_call(
        hand_over,
        out_shape=[jax.ShapeDtypeStruct((2 * rows, HALF), F32)] * 4,
        in_specs=[pl.BlockSpec(memory_space=pl.ANY)] * 4,
        out_specs=[pl.BlockSpec(memory_space=pl.ANY)] * 4,
        scratch_shapes=[pltpu.VMEM((4, 2 * rows, HALF), F32), pltpu.SemaphoreType.DMA((8,))],
        compiler_params=pltpu.CompilerParams(vmem_limit_bytes=56 * 1024 * 1024),
    )(*outs)
    return (
        outs[0].reshape(rows, 1, width),
        outs[1].reshape(rows, 1, width),
        outs[2].reshape(1, rows, 1, width),
        outs[3].reshape(1, rows, 1, width),
    )


def solution(mesh):
    placed = (
        P("vintage", "tile", "freq", None, None),
        P("freq", "tile", None),
        P("freq", "tile", None),
        P("vintage", "freq", "tile", None),
        P("vintage", "freq", "tile", None),
        P(None, None, "freq", None),
        P(None, None, "freq"),
        P("vintage", "tile", "freq", None),
        P("vintage", "tile", "freq", None),
    )
    return jax.shard_map(
        per_device,
        mesh=mesh,
        in_specs=placed,
        out_specs=(
            P("freq", "tile", None),
            P("freq", "tile", None),
            P("vintage", "freq", "tile", None),
            P("vintage", "freq", "tile", None),
        ),
        check_vma=False,
    )
```

```python
import jax
import jax.numpy as jnp
from jax import lax
from jax.experimental import pallas as pl
from jax.experimental.pallas import tpu as pltpu
from jax.sharding import PartitionSpec as P

MESH = pl.DeviceIdType.MESH
BF16, F32 = jnp.bfloat16, jnp.float32

step_size = 8.0
shrink = 0.5

NZ, NY = 16, 4
EXT = 512
NB = 32
HALF = 128
NEAR = 3
FAR = NZ // 2 - NEAR
SIGNS = (1, -1)
HALVES = (pl.ds(0, NB // 2), pl.ds(NB // 2, NB // 2))
ROWS = (pl.ds(0, NB * 8), pl.ds(NB * 8, NB * 8))


def place(rel):
    if abs(rel) == NZ // 2:
        return 0
    far = 2 * (NZ // 2 - abs(rel))
    return far - 1 if rel >= 0 else far


def far_count(sign, side):
    return FAR if (sign > 0) == (side == 0) else FAR - 1


def dot(a, b, ca=1, cb=0):
    return lax.dot_general(a, b, (((ca,), (cb,)), ((), ())), preferred_element_type=F32)


def kernel(
    pairs,
    live,
    observed,
    common_left,
    common_right,
    innov_left,
    innov_right,
    row_mask,
    col_mask,
    out_common_left,
    out_common_right,
    out_innov_left,
    out_innov_right,
    s,
):
    v = lax.axis_index("vintage")
    t = lax.axis_index("tile")
    z, y = t // NY, t % NY

    def along_z(d):
        return {"tile": lax.rem(z + d + NZ, NZ) * NY + y}

    def along_y(d):
        return {"tile": z * NY + lax.rem(y + d + NY, NY)}

    partner = {"vintage": 1 - v}

    barrier = pltpu.get_barrier_semaphore()
    peers = [along_z(sg * e) for e in range(1, max(FAR, 1) + 1) for sg in SIGNS]
    peers += [along_y(k) for k in range(1, NY)] + [partner]
    for peer in peers:
        pl.semaphore_signal(barrier, inc=1, device_id=peer, device_id_type=MESH)

    load_obs = pltpu.make_async_copy(observed.at[0, 0], s["obs"], s["local_sem"].at[0])
    load_obs.start()

    started, gone = [], set()

    def leave(copies):
        for copy in copies:
            copy.wait_send()
            gone.add(id(copy))

    def send(src, dst, dev):
        i = len(started)
        copy = pltpu.make_async_remote_copy(
            src_ref=src,
            dst_ref=dst,
            send_sem=s["send"].at[i],
            recv_sem=s["recv"].at[i],
            device_id=dev,
            device_id_type=MESH,
        )
        copy.start()
        started.append(copy)
        return copy

    def pick(rel, k, slot, side):
        owner = lax.rem(z + rel + NZ, NZ) * NY + lax.rem(y + k, NY)
        return pairs[v, slot, side, owner]

    commons = (common_left, common_right)
    innovs = (innov_left, innov_right)
    for side in range(2):
        for src, dst in ((commons[side], s["common"][side]), (innovs[side], s["innov"][side])):
            x = src[...].astype(F32)
            dst[pl.ds(0, NB * 8, 2), :] = x[:, :HALF]
            dst[pl.ds(1, NB * 8, 2), :] = x[:, HALF:]
        joined = (s["common"][side][...] + s["innov"][side][...]).astype(BF16)
        s["own"][side][...] = joined.reshape(NB, 16, HALF)

    pl.semaphore_wait(barrier, len(peers))

    dense = {}

    def first_hop(side):
        for c, blocks in enumerate(HALVES):
            for g, sign in enumerate(SIGNS):
                dense[g, 1, side, c] = send(
                    s["own"][side].at[blocks], s["dense"][g][0][side].at[blocks], along_z(sign)
                )

    first_hop(0)

    def choose(bufs, o):
        for k in range(NY):
            for side in range(2):
                for slot in range(2):
                    piece = bufs[side][pick(0, k, slot, side)]
                    if k == 0:
                        s["g"][slot, 0, o, side] = piece
                    else:
                        s["ysend"][slot, k - 1, o, side] = piece

    def spread(slots, o0, n):
        return [
            send(
                s["ysend"].at[slots, k - 1, pl.ds(o0, n)],
                s["g"].at[slots, k, pl.ds(o0, n)],
                along_y(k),
            )
            for k in range(1, NY)
        ]

    both_slots = pl.ds(0, 2)

    def build_order():
        row = lax.broadcasted_iota(jnp.int32, (EXT, HALF), 0)
        lane = lax.broadcasted_iota(jnp.int32, (EXT, HALF), 1)
        k, o, j = row >> 7, (row >> 3) & 15, row & 7
        dist = NZ // 2 - ((o + 1) >> 1)
        rel = jnp.where((o & 1) == 1, dist, -dist)
        target = 64 * j + ((z + rel + NZ) & (NZ - 1)) * NY + ((y - k + NY) & (NY - 1))
        for c in range(EXT // HALF):
            s["order"][:, c * HALF : (c + 1) * HALF] = jnp.where(
                target == lane + c * HALF, 1.0, 0.0
            ).astype(BF16)

    def order_tile(slot):
        order = s["order"][...]
        turned = dot(order, s["obs"][slot]).astype(BF16)
        for h in range(2):
            cols = slice(h * EXT, (h + 1) * EXT)
            s["obs_o"][slot, :, cols] = dot(turned[:, cols], order, 1, 1).astype(BF16)

    def order_masks(slot):
        order = s["order"][...]
        rows = jnp.broadcast_to(row_mask[slot : slot + 1, :].astype(F32), (HALF, EXT)).astype(BF16)
        cols = jnp.broadcast_to(col_mask[slot : slot + 1, :].astype(F32), (16, EXT)).astype(BF16)
        by_row = dot(order, rows, 1, 1)
        by_col = dot(cols, order, 1, 1)[0:1, :]
        weight = jnp.concatenate([by_row] * (EXT // HALF), axis=1) * by_col
        s["weight"][slot] = (weight * live[v, slot, t].astype(F32)).astype(BF16)

    def one_hot(rel, side):
        row = lax.broadcasted_iota(jnp.int32, (NB * 16, HALF), 0)
        lane = lax.broadcasted_iota(jnp.int32, (1, HALF), 1)
        target = jnp.zeros((1, HALF), jnp.int32)
        for slot in range(2):
            for k in range(NY):
                target = jnp.where(
                    (lane >> 4) == slot * NY + k, pick(rel, k, slot, side), target
                )
        return jnp.where(row == target * 16 + (lane & 15), 1.0, 0.0).astype(BF16)

    def build_own_hot():
        for side in range(2):
            hot = one_hot(0, side)
            s["hot"][side][...] = hot
            for g in range(2):
                s["hot_far"][g][side][:, :HALF] = hot

    def build_far_hot(g):
        sign = SIGNS[g]
        for side in range(2):
            for e in range(1, far_count(sign, side) + 1):
                s["hot_far"][g][side][:, e * HALF : (e + 1) * HALF] = one_hot(-sign * e, side)

    choose(s["own"], place(0))
    near = spread(both_slots, place(0), 1)
    build_order()
    leave([dense[g, 1, 0, c] for c in range(2) for g in range(2)])
    first_hop(1)

    picks = {}

    def stage_far(g, side, slot):
        here = s["dense"][g][NEAR - 1][side]
        for e in range(far_count(SIGNS[g], side), 0, -1):
            for k in range(NY):
                s["far_send"][g][side][slot, e - 1, k] = here[pick(SIGNS[g] * e, k, slot, side)]

    def send_far(side, slot):
        for e in range(FAR, 0, -1):
            for g, sign in enumerate(SIGNS):
                if e <= far_count(sign, side):
                    picks[g, e, side, slot] = send(
                        s["far_send"][g][side].at[slot, e - 1],
                        s["far"][g][side].at[slot, e - 1],
                        along_z(sign * e),
                    )

    for h in range(1, NEAR + 1):
        for side in range(2):
            for c, blocks in enumerate(HALVES):
                for g, sign in enumerate(SIGNS):
                    dense[g, h, side, c].wait_recv()
                    if h < NEAR:
                        dense[g, h + 1, side, c] = send(
                            s["dense"][g][h - 1][side].at[blocks],
                            s["dense"][g][h][side].at[blocks],
                            along_z(sign),
                        )
            if h == NEAR:
                for g in range(2):
                    stage_far(g, side, 0)
                send_far(side, 0)
        for g, sign in enumerate(SIGNS):
            choose(s["dense"][g][h - 1], place(-sign * h))
        near += spread(both_slots, place(h), 2)
    for side in range(2):
        for g in range(2):
            stage_far(g, side, 1)
    load_obs.wait()
    order_tile(0)
    leave([picks[key] for key in picks if key[3] == 0])
    for side in range(2):
        send_far(side, 1)
    order_masks(0)
    order_tile(1)
    order_masks(1)

    def far_in(slot):
        copies = []
        for e in range(FAR, 0, -1):
            d = NEAR + e
            for g, sign in enumerate(SIGNS):
                for side in range(2):
                    if e <= far_count(sign, side):
                        picks[g, e, side, slot].wait_recv()
                        o = place(-sign * d)
                        s["g"][slot, 0, o, side] = s["far"][g][side][slot, e - 1, 0]
                        for k in range(1, NY):
                            s["ysend"][slot, k - 1, o, side] = s["far"][g][side][slot, e - 1, k]
            copies += spread(slot, place(d), 1 if d == NZ // 2 else 2)
        return copies

    def parts(side, slot):
        x = s["g"][slot, :, :, side].reshape(2 * EXT, HALF).astype(F32)
        s["wide"][side][...] = x
        real = s["wide"][side][pl.ds(0, EXT, 2), :].astype(BF16)
        imag = s["wide"][side][pl.ds(1, EXT, 2), :].astype(BF16)
        return real, imag

    def keep(delta, side, slot):
        s["wide"][side][pl.ds(0, EXT, 2), :] = delta[:, :HALF]
        s["wide"][side][pl.ds(1, EXT, 2), :] = delta[:, HALF:]
        pieces = s["wide"][side][...].astype(BF16).reshape(NY, NZ, 16, HALF)
        s["q"][slot, 0, side] = pieces[0]
        for k in range(1, NY):
            s["back"][slot, k - 1, side] = pieces[k]

    back = {}

    def give_back(slot, i, sides, o0, n):
        for k in (2, 1, 3):
            back[slot, i, k] = send(
                s["back"].at[slot, k - 1, sides, pl.ds(o0, n)],
                s["q"].at[slot, k, sides, pl.ds(o0, n)],
                along_y(-k),
            )

    scale = 1.0 / EXT

    def tile(slot):
        a_re, a_im = parts(0, slot)
        b_re, b_im = parts(1, slot)
        a = jnp.concatenate([a_re, a_im], axis=1)
        s_re = jnp.concatenate([b_re, -b_im], axis=1)
        s_im = jnp.concatenate([b_im, b_re], axis=1)
        t_re = jnp.concatenate([a_re, -a_im], axis=1)
        t_im = jnp.concatenate([a_im, a_re], axis=1)
        weight = s["weight"][slot].astype(F32)
        m_re = (weight * (dot(a, s_re, 1, 1) - s["obs_o"][slot, :, :EXT].astype(F32))).astype(BF16)
        m_im = (weight * (dot(a, s_im, 1, 1) - s["obs_o"][slot, :, EXT:].astype(F32))).astype(BF16)
        keep((dot(m_re, s_re) + dot(m_im, s_im)) * scale, 0, slot)
        give_back(slot, 0, 0, 0, 2 * FAR - 1)
        keep((dot(m_re, t_re, 0, 0) + dot(m_im, t_im, 0, 0)) * scale, 1, slot)
        give_back(slot, 1, 1, 0, 2 * FAR - 1)
        give_back(slot, 2, pl.ds(0, 2), 2 * FAR - 1, 4)
        give_back(slot, 3, pl.ds(0, 2), 2 * FAR + 3, 2 * NEAR - 3)

    def arrived(slot, i):
        for k in range(1, NY):
            back[slot, i, k].wait_recv()

    def own_picks(rel, side):
        return s["q"][:, :, side, place(rel)].reshape(HALF, HALF)

    raw = {}

    def far_out(slot):
        for side in range(2):
            arrived(slot, side)
            for e in range(FAR, 0, -1):
                for g, sign in enumerate(SIGNS):
                    if e <= far_count(sign, side):
                        rows = pl.ds(e * HALF + slot * (HALF // 2), HALF // 2)
                        mine = s["q"][slot, :, side, place(sign * (NEAR + e))]
                        s["raw_send"][g][side][rows, :] = mine.reshape(HALF // 2, HALF)
                        raw[g, e, side, slot] = send(
                            s["raw_send"][g][side].at[rows],
                            s["raw"][g][side].at[rows],
                            along_z(sign * e),
                        )

    early = far_in(0)
    for copy in near + early:
        copy.wait_recv()
    tile(0)
    build_own_hot()
    late = far_in(1)
    far_out(0)
    for copy in late:
        copy.wait_recv()
    tile(1)
    far_out(1)
    for g in range(2):
        build_far_hot(g)
    for slot in range(2):
        arrived(slot, 2)
    for g, sign in enumerate(SIGNS):
        for side in range(2):
            s["raw"][g][side][0:HALF, :] = own_picks(sign * NEAR, side)

    def own_sums(h):
        for side in range(2):
            both = jnp.concatenate([own_picks(h, side), own_picks(-h, side)], axis=1)
            s["add"][h - 1][side][...] = dot(s["hot"][side][...], both)

    own_sums(NEAR - 1)
    chain = {}

    def pass_on(g, h, side, c):
        chain[g, h, side, c] = send(
            s["sum_send"][g][h][side].at[ROWS[c]], s["sum"][g][h][side].at[ROWS[c]], along_z(SIGNS[g])
        )

    for side in range(2):
        for g, sign in enumerate(SIGNS):
            for slot in range(2):
                for e in range(far_count(sign, side), 0, -1):
                    raw[g, e, side, slot].wait_recv()
        for c, rows in enumerate(ROWS):
            for g, sign in enumerate(SIGNS):
                depth = (far_count(sign, side) + 1) * HALF
                total = dot(s["hot_far"][g][side][rows, :depth], s["raw"][g][side][0:depth, :])
                s["sum_send"][g][NEAR - 1][side][rows, :] = total.astype(BF16)
                if side == 1:
                    leave([chain[g, NEAR - 1, 0, c]])
                pass_on(g, NEAR - 1, side, c)
    for slot in range(2):
        arrived(slot, 3)
    for h in range(NEAR - 2, 0, -1):
        own_sums(h)
    for side in range(2):
        s["grad"][side][...] = dot(s["hot"][side][...], own_picks(0, side))
    for h in range(NEAR - 1, 0, -1):
        for side in range(2):
            for c, rows in enumerate(ROWS):
                for g in range(2):
                    chain[g, h, side, c].wait_recv()
                    total = s["sum"][g][h][side][rows, :].astype(F32)
                    total = total + s["add"][h - 1][side][rows, g * HALF : (g + 1) * HALF]
                    s["sum_send"][g][h - 1][side][rows, :] = total.astype(BF16)
                    pass_on(g, h - 1, side, c)
    swap = {}
    for side in range(2):
        for c, rows in enumerate(ROWS):
            for g in range(2):
                chain[g, 0, side, c].wait_recv()
            s["grad"][side][rows, :] = (
                s["grad"][side][rows, :]
                + s["sum"][0][0][side][rows, :].astype(F32)
                + s["sum"][1][0][side][rows, :].astype(F32)
            )
            swap[side, c] = send(s["grad"][side].at[rows], s["other"][side].at[rows], partner)
        innov = s["innov"][side][...]
        out = (out_innov_left, out_innov_right)[side]
        out[...] = innov - step_size * (s["grad"][side][...] + shrink * innov)
    for side, out in enumerate((out_common_left, out_common_right)):
        for c, rows in enumerate(ROWS):
            swap[side, c].wait_recv()
            out[rows, :] = s["common"][side][rows, :] - step_size * (
                s["grad"][side][rows, :] + s["other"][side][rows, :]
            )
    leave([copy for copy in started if id(copy) not in gone])


def hand_over(*refs):
    given, outs, held, sems = refs[:4], refs[4:8], refs[8], refs[9]
    inward = [pltpu.make_async_copy(given[i], held.at[i], sems.at[i]) for i in range(4)]
    outward = [pltpu.make_async_copy(held.at[i], outs[i], sems.at[4 + i]) for i in range(4)]
    for copy in inward:
        copy.start()
    for i in range(4):
        inward[i].wait()
        outward[i].start()
    for copy in outward:
        copy.wait()


def shard(dtype=BF16):
    return pltpu.VMEM((NB * 16, HALF), dtype)


def scratch():
    blocks = pltpu.VMEM((NB, 16, HALF), BF16)
    exchange = (NZ, 2, 16, HALF)
    copies = 16 * NEAR + 4 * (4 * FAR - 2) + (NEAR + 2 * FAR + 1) * 3 + 24 + 4
    far = [
        [pltpu.VMEM((2, far_count(sign, side), NY, 16, HALF), BF16) for side in range(2)]
        for sign in SIGNS
    ]
    raw = [
        [pltpu.VMEM(((far_count(sign, side) + 1) * HALF, HALF), BF16) for side in range(2)]
        for sign in SIGNS
    ]
    hot_far = [
        [pltpu.VMEM((NB * 16, (far_count(sign, side) + 1) * HALF), BF16) for side in range(2)]
        for sign in SIGNS
    ]
    return {
        "common": [shard(F32)] * 2,
        "innov": [shard(F32)] * 2,
        "grad": [shard(F32)] * 2,
        "other": [shard(F32)] * 2,
        "own": [blocks] * 2,
        "dense": [[[blocks] * 2 for _ in range(NEAR)] for _ in range(2)],
        "far_send": far,
        "far": far,
        "ysend": pltpu.VMEM((2, NY - 1) + exchange, BF16),
        "g": pltpu.VMEM((2, NY) + exchange, BF16),
        "obs": pltpu.VMEM((2, EXT, 2 * EXT), BF16),
        "obs_o": pltpu.VMEM((2, EXT, 2 * EXT), BF16),
        "order": pltpu.VMEM((EXT, EXT), BF16),
        "weight": pltpu.VMEM((2, EXT, EXT), BF16),
        "hot": [shard()] * 2,
        "hot_far": hot_far,
        "wide": [pltpu.VMEM((2 * EXT, HALF), F32)] * 2,
        "back": pltpu.VMEM((2, NY - 1, 2, NZ, 16, HALF), BF16),
        "q": pltpu.VMEM((2, NY, 2, NZ, 16, HALF), BF16),
        "raw_send": raw,
        "raw": raw,
        "sum_send": [[[shard()] * 2 for _ in range(NEAR)] for _ in range(2)],
        "sum": [[[shard()] * 2 for _ in range(NEAR)] for _ in range(2)],
        "add": [[pltpu.VMEM((NB * 16, 2 * HALF), F32)] * 2 for _ in range(NEAR - 1)],
        "send": pltpu.SemaphoreType.DMA((copies,)),
        "recv": pltpu.SemaphoreType.DMA((copies,)),
        "local_sem": pltpu.SemaphoreType.DMA((1,)),
    }


def per_device(
    observed,
    common_left,
    common_right,
    innov_left,
    innov_right,
    tile_block_pairs,
    live,
    row_mask,
    col_mask,
):
    rows, width = common_left.shape[0], common_left.shape[2]
    vmem = pl.BlockSpec(memory_space=pltpu.VMEM)
    smem = pl.BlockSpec(memory_space=pltpu.SMEM)
    outs = pl.pallas_call(
        kernel,
        out_shape=[jax.ShapeDtypeStruct((2 * rows, HALF), F32)] * 4,
        in_specs=[smem, smem, pl.BlockSpec(memory_space=pl.ANY)] + [vmem] * 6,
        out_specs=[vmem] * 4,
        scratch_shapes=[scratch()],
        compiler_params=pltpu.CompilerParams(
            collective_id=0, has_side_effects=True, vmem_limit_bytes=56 * 1024 * 1024
        ),
    )(
        tile_block_pairs.transpose(0, 2, 3, 1),
        live.transpose(0, 2, 1),
        observed,
        common_left.reshape(rows, width),
        common_right.reshape(rows, width),
        innov_left.reshape(rows, width),
        innov_right.reshape(rows, width),
        row_mask.reshape(2, EXT),
        col_mask.reshape(2, EXT),
    )
    outs = pl.pallas_call(
        hand_over,
        out_shape=[jax.ShapeDtypeStruct((2 * rows, HALF), F32)] * 4,
        in_specs=[pl.BlockSpec(memory_space=pl.ANY)] * 4,
        out_specs=[pl.BlockSpec(memory_space=pl.ANY)] * 4,
        scratch_shapes=[pltpu.VMEM((4, 2 * rows, HALF), F32), pltpu.SemaphoreType.DMA((8,))],
        compiler_params=pltpu.CompilerParams(vmem_limit_bytes=56 * 1024 * 1024),
    )(*outs)
    return (
        outs[0].reshape(rows, 1, width),
        outs[1].reshape(rows, 1, width),
        outs[2].reshape(1, rows, 1, width),
        outs[3].reshape(1, rows, 1, width),
    )


def solution(mesh):
    placed = (
        P("vintage", "tile", "freq", None, None),
        P("freq", "tile", None),
        P("freq", "tile", None),
        P("vintage", "freq", "tile", None),
        P("vintage", "freq", "tile", None),
        P(None, None, "freq", None),
        P(None, None, "freq"),
        P("vintage", "tile", "freq", None),
        P("vintage", "tile", "freq", None),
    )
    return jax.shard_map(
        per_device,
        mesh=mesh,
        in_specs=placed,
        out_specs=(
            P("freq", "tile", None),
            P("freq", "tile", None),
            P("vintage", "freq", "tile", None),
            P("vintage", "freq", "tile", None),
        ),
        check_vma=False,
    )
```

```python
import jax
import jax.numpy as jnp
from jax import lax
from jax.experimental import pallas as pl
from jax.experimental.pallas import tpu as pltpu
from jax.sharding import PartitionSpec as P

MESH = pl.DeviceIdType.MESH
BF16, F32 = jnp.bfloat16, jnp.float32

step_size = 8.0
shrink = 0.5

NZ, NY = 16, 4
EXT = 512
NB = 32
HALF = 128
NEAR = 3
FAR = NZ // 2 - NEAR
SIGNS = (1, -1)
HALVES = (pl.ds(0, NB // 2), pl.ds(NB // 2, NB // 2))
ROWS = (pl.ds(0, NB * 8), pl.ds(NB * 8, NB * 8))


def place(rel):
    if abs(rel) == NZ // 2:
        return 0
    far = 2 * (NZ // 2 - abs(rel))
    return far - 1 if rel >= 0 else far


def far_count(sign, side):
    return FAR if (sign > 0) == (side == 0) else FAR - 1


def dot(a, b, ca=1, cb=0):
    return lax.dot_general(a, b, (((ca,), (cb,)), ((), ())), preferred_element_type=F32)


def kernel(
    pairs,
    live,
    observed,
    common_left,
    common_right,
    innov_left,
    innov_right,
    row_mask,
    col_mask,
    out_common_left,
    out_common_right,
    out_innov_left,
    out_innov_right,
    s,
):
    v = lax.axis_index("vintage")
    t = lax.axis_index("tile")
    z, y = t // NY, t % NY

    def along_z(d):
        return {"tile": lax.rem(z + d + NZ, NZ) * NY + y}

    def along_y(d):
        return {"tile": z * NY + lax.rem(y + d + NY, NY)}

    partner = {"vintage": 1 - v}

    barrier = pltpu.get_barrier_semaphore()
    peers = [along_z(sg * e) for e in range(1, max(FAR, 1) + 1) for sg in SIGNS]
    peers += [along_y(k) for k in range(1, NY)] + [partner]
    for peer in peers:
        pl.semaphore_signal(barrier, inc=1, device_id=peer, device_id_type=MESH)

    load_obs = pltpu.make_async_copy(observed.at[0, 0], s["obs"], s["local_sem"].at[0])
    load_obs.start()

    started, gone = [], set()

    def leave(copies):
        for copy in copies:
            copy.wait_send()
            gone.add(id(copy))

    def send(src, dst, dev):
        i = len(started)
        copy = pltpu.make_async_remote_copy(
            src_ref=src,
            dst_ref=dst,
            send_sem=s["send"].at[i],
            recv_sem=s["recv"].at[i],
            device_id=dev,
            device_id_type=MESH,
        )
        copy.start()
        started.append(copy)
        return copy

    def pick(rel, k, slot, side):
        owner = lax.rem(z + rel + NZ, NZ) * NY + lax.rem(y + k, NY)
        return pairs[v, slot, side, owner]

    commons = (common_left, common_right)
    innovs = (innov_left, innov_right)

    def prepare(side):
        for src, dst in ((commons[side], s["common"][side]), (innovs[side], s["innov"][side])):
            x = src[...].astype(F32)
            dst[pl.ds(0, NB * 8, 2), :] = x[:, :HALF]
            dst[pl.ds(1, NB * 8, 2), :] = x[:, HALF:]
        joined = (s["common"][side][...] + s["innov"][side][...]).astype(BF16)
        s["own"][side][...] = joined.reshape(NB, 16, HALF)

    prepare(0)
    pl.semaphore_wait(barrier, len(peers))

    dense = {}

    def first_hop(side):
        for c, blocks in enumerate(HALVES):
            for g, sign in enumerate(SIGNS):
                dense[g, 1, side, c] = send(
                    s["own"][side].at[blocks], s["dense"][g][0][side].at[blocks], along_z(sign)
                )

    first_hop(0)
    prepare(1)

    def choose(bufs, o):
        for k in range(NY):
            for side in range(2):
                for slot in range(2):
                    piece = bufs[side][pick(0, k, slot, side)]
                    if k == 0:
                        s["g"][slot, 0, o, side] = piece
                    else:
                        s["ysend"][slot, k - 1, o, side] = piece

    def spread(slots, o0, n):
        return [
            send(
                s["ysend"].at[slots, k - 1, pl.ds(o0, n)],
                s["g"].at[slots, k, pl.ds(o0, n)],
                along_y(k),
            )
            for k in range(1, NY)
        ]

    both_slots = pl.ds(0, 2)

    def build_order():
        row = lax.broadcasted_iota(jnp.int32, (EXT, HALF), 0)
        lane = lax.broadcasted_iota(jnp.int32, (EXT, HALF), 1)
        k, o, j = row >> 7, (row >> 3) & 15, row & 7
        dist = NZ // 2 - ((o + 1) >> 1)
        rel = jnp.where((o & 1) == 1, dist, -dist)
        target = 64 * j + ((z + rel + NZ) & (NZ - 1)) * NY + ((y - k + NY) & (NY - 1))
        for c in range(EXT // HALF):
            s["order"][:, c * HALF : (c + 1) * HALF] = jnp.where(
                target == lane + c * HALF, 1.0, 0.0
            ).astype(BF16)

    def order_tile(slot):
        order = s["order"][...]
        turned = dot(order, s["obs"][slot]).astype(BF16)
        for h in range(2):
            cols = slice(h * EXT, (h + 1) * EXT)
            s["obs_o"][slot, :, cols] = dot(turned[:, cols], order, 1, 1).astype(BF16)

    def order_masks(slot):
        order = s["order"][...]
        rows = jnp.broadcast_to(row_mask[slot : slot + 1, :].astype(F32), (HALF, EXT)).astype(BF16)
        cols = jnp.broadcast_to(col_mask[slot : slot + 1, :].astype(F32), (16, EXT)).astype(BF16)
        by_row = dot(order, rows, 1, 1)
        by_col = dot(cols, order, 1, 1)[0:1, :]
        weight = jnp.concatenate([by_row] * (EXT // HALF), axis=1) * by_col
        s["weight"][slot] = (weight * live[v, slot, t].astype(F32)).astype(BF16)

    def one_hot(rel, side):
        row = lax.broadcasted_iota(jnp.int32, (NB * 16, HALF), 0)
        lane = lax.broadcasted_iota(jnp.int32, (1, HALF), 1)
        target = jnp.zeros((1, HALF), jnp.int32)
        for slot in range(2):
            for k in range(NY):
                target = jnp.where(
                    (lane >> 4) == slot * NY + k, pick(rel, k, slot, side), target
                )
        return jnp.where(row == target * 16 + (lane & 15), 1.0, 0.0).astype(BF16)

    def build_own_hot():
        for side in range(2):
            hot = one_hot(0, side)
            s["hot"][side][...] = hot
            for g in range(2):
                s["hot_far"][g][side][:, :HALF] = hot

    def build_far_hot(g):
        sign = SIGNS[g]
        for side in range(2):
            for e in range(1, far_count(sign, side) + 1):
                s["hot_far"][g][side][:, e * HALF : (e + 1) * HALF] = one_hot(-sign * e, side)

    choose(s["own"], place(0))
    near = spread(both_slots, place(0), 1)
    build_order()
    leave([dense[g, 1, 0, c] for c in range(2) for g in range(2)])
    first_hop(1)

    picks = {}

    def stage_far(g, side, slot):
        here = s["dense"][g][NEAR - 1][side]
        for e in range(far_count(SIGNS[g], side), 0, -1):
            for k in range(NY):
                s["far_send"][g][side][slot, e - 1, k] = here[pick(SIGNS[g] * e, k, slot, side)]

    def send_far(side, slot):
        for e in range(FAR, 0, -1):
            for g, sign in enumerate(SIGNS):
                if e <= far_count(sign, side):
                    picks[g, e, side, slot] = send(
                        s["far_send"][g][side].at[slot, e - 1],
                        s["far"][g][side].at[slot, e - 1],
                        along_z(sign * e),
                    )

    for h in range(1, NEAR + 1):
        for side in range(2):
            for c, blocks in enumerate(HALVES):
                for g, sign in enumerate(SIGNS):
                    dense[g, h, side, c].wait_recv()
                    if h < NEAR:
                        dense[g, h + 1, side, c] = send(
                            s["dense"][g][h - 1][side].at[blocks],
                            s["dense"][g][h][side].at[blocks],
                            along_z(sign),
                        )
            if h == NEAR:
                for g in range(2):
                    stage_far(g, side, 0)
                send_far(side, 0)
        for g, sign in enumerate(SIGNS):
            choose(s["dense"][g][h - 1], place(-sign * h))
        near += spread(both_slots, place(h), 2)
    for side in range(2):
        for g in range(2):
            stage_far(g, side, 1)
    load_obs.wait()
    order_tile(0)
    order_masks(0)
    leave([picks[key] for key in picks if key[3] == 0])
    for side in range(2):
        send_far(side, 1)
    def far_in(slot):
        copies = []
        for e in range(FAR, 0, -1):
            d = NEAR + e
            for g, sign in enumerate(SIGNS):
                for side in range(2):
                    if e <= far_count(sign, side):
                        picks[g, e, side, slot].wait_recv()
                        o = place(-sign * d)
                        s["g"][slot, 0, o, side] = s["far"][g][side][slot, e - 1, 0]
                        for k in range(1, NY):
                            s["ysend"][slot, k - 1, o, side] = s["far"][g][side][slot, e - 1, k]
            copies += spread(slot, place(d), 1 if d == NZ // 2 else 2)
        return copies

    def parts(side, slot):
        x = s["g"][slot, :, :, side].reshape(2 * EXT, HALF).astype(F32)
        s["wide"][side][...] = x
        real = s["wide"][side][pl.ds(0, EXT, 2), :].astype(BF16)
        imag = s["wide"][side][pl.ds(1, EXT, 2), :].astype(BF16)
        return real, imag

    def keep(delta, side, slot):
        s["wide"][side][pl.ds(0, EXT, 2), :] = delta[:, :HALF]
        s["wide"][side][pl.ds(1, EXT, 2), :] = delta[:, HALF:]
        pieces = s["wide"][side][...].astype(BF16).reshape(NY, NZ, 16, HALF)
        s["q"][slot, 0, side] = pieces[0]
        for k in range(1, NY):
            s["back"][slot, k - 1, side] = pieces[k]

    back = {}

    def give_back(slot, i, sides, o0, n):
        for k in (2, 1, 3):
            back[slot, i, k] = send(
                s["back"].at[slot, k - 1, sides, pl.ds(o0, n)],
                s["q"].at[slot, k, sides, pl.ds(o0, n)],
                along_y(-k),
            )

    scale = 1.0 / EXT

    def tile(slot):
        a_re, a_im = parts(0, slot)
        b_re, b_im = parts(1, slot)
        a = jnp.concatenate([a_re, a_im], axis=1)
        s_re = jnp.concatenate([b_re, -b_im], axis=1)
        s_im = jnp.concatenate([b_im, b_re], axis=1)
        t_re = jnp.concatenate([a_re, -a_im], axis=1)
        t_im = jnp.concatenate([a_im, a_re], axis=1)
        weight = s["weight"][slot].astype(F32)
        m_re = (weight * (dot(a, s_re, 1, 1) - s["obs_o"][slot, :, :EXT].astype(F32))).astype(BF16)
        m_im = (weight * (dot(a, s_im, 1, 1) - s["obs_o"][slot, :, EXT:].astype(F32))).astype(BF16)
        keep((dot(m_re, s_re) + dot(m_im, s_im)) * scale, 0, slot)
        give_back(slot, 0, 0, 0, 2 * FAR - 1)
        keep((dot(m_re, t_re, 0, 0) + dot(m_im, t_im, 0, 0)) * scale, 1, slot)
        give_back(slot, 1, 1, 0, 2 * FAR - 1)
        give_back(slot, 2, pl.ds(0, 2), 2 * FAR - 1, 4)
        give_back(slot, 3, pl.ds(0, 2), 2 * FAR + 3, 2 * NEAR - 3)

    def arrived(slot, i):
        for k in range(1, NY):
            back[slot, i, k].wait_recv()

    def own_picks(rel, side):
        return s["q"][:, :, side, place(rel)].reshape(HALF, HALF)

    raw = {}

    def far_out(slot, side):
        arrived(slot, side)
        for e in range(FAR, 0, -1):
            for g, sign in enumerate(SIGNS):
                if e <= far_count(sign, side):
                    rows = pl.ds(e * HALF + slot * (HALF // 2), HALF // 2)
                    mine = s["q"][slot, :, side, place(sign * (NEAR + e))]
                    s["raw_send"][g][side][rows, :] = mine.reshape(HALF // 2, HALF)
                    raw[g, e, side, slot] = send(
                        s["raw_send"][g][side].at[rows], s["raw"][g][side].at[rows], along_z(sign * e)
                    )

    early = far_in(0)
    order_tile(1)
    order_masks(1)
    for copy in near + early:
        copy.wait_recv()
    tile(0)
    build_own_hot()
    far_out(0, 0)
    late = far_in(1)
    far_out(0, 1)
    for copy in late:
        copy.wait_recv()
    tile(1)
    far_out(1, 0)
    far_out(1, 1)
    for g in range(2):
        build_far_hot(g)
    for slot in range(2):
        arrived(slot, 2)
    for g, sign in enumerate(SIGNS):
        for side in range(2):
            s["raw"][g][side][0:HALF, :] = own_picks(sign * NEAR, side)

    def own_sums(h):
        for side in range(2):
            both = jnp.concatenate([own_picks(h, side), own_picks(-h, side)], axis=1)
            s["add"][h - 1][side][...] = dot(s["hot"][side][...], both)

    own_sums(NEAR - 1)
    chain = {}

    def pass_on(g, h, side, c):
        chain[g, h, side, c] = send(
            s["sum_send"][g][h][side].at[ROWS[c]], s["sum"][g][h][side].at[ROWS[c]], along_z(SIGNS[g])
        )

    for side in range(2):
        for g, sign in enumerate(SIGNS):
            for slot in range(2):
                for e in range(far_count(sign, side), 0, -1):
                    raw[g, e, side, slot].wait_recv()
        for c, rows in enumerate(ROWS):
            for g, sign in enumerate(SIGNS):
                depth = (far_count(sign, side) + 1) * HALF
                total = dot(s["hot_far"][g][side][rows, :depth], s["raw"][g][side][0:depth, :])
                s["sum_send"][g][NEAR - 1][side][rows, :] = total.astype(BF16)
                if side == 1:
                    leave([chain[g, NEAR - 1, 0, c]])
                pass_on(g, NEAR - 1, side, c)
    for slot in range(2):
        arrived(slot, 3)
    for h in range(NEAR - 2, 0, -1):
        own_sums(h)
    for side in range(2):
        s["grad"][side][...] = dot(s["hot"][side][...], own_picks(0, side))
    for h in range(NEAR - 1, 0, -1):
        for side in range(2):
            for c, rows in enumerate(ROWS):
                for g in range(2):
                    chain[g, h, side, c].wait_recv()
                    total = s["sum"][g][h][side][rows, :].astype(F32)
                    total = total + s["add"][h - 1][side][rows, g * HALF : (g + 1) * HALF]
                    s["sum_send"][g][h - 1][side][rows, :] = total.astype(BF16)
                    pass_on(g, h - 1, side, c)
    swap = {}
    for side in range(2):
        for c, rows in enumerate(ROWS):
            for g in range(2):
                chain[g, 0, side, c].wait_recv()
            s["grad"][side][rows, :] = (
                s["grad"][side][rows, :]
                + s["sum"][0][0][side][rows, :].astype(F32)
                + s["sum"][1][0][side][rows, :].astype(F32)
            )
            swap[side, c] = send(s["grad"][side].at[rows], s["other"][side].at[rows], partner)
        innov = s["innov"][side][...]
        out = (out_innov_left, out_innov_right)[side]
        out[...] = innov - step_size * (s["grad"][side][...] + shrink * innov)
    for side, out in enumerate((out_common_left, out_common_right)):
        for c, rows in enumerate(ROWS):
            swap[side, c].wait_recv()
            out[rows, :] = s["common"][side][rows, :] - step_size * (
                s["grad"][side][rows, :] + s["other"][side][rows, :]
            )
    leave([copy for copy in started if id(copy) not in gone])


def hand_over(*refs):
    given, outs, held, sems = refs[:4], refs[4:8], refs[8], refs[9]
    inward = [pltpu.make_async_copy(given[i], held.at[i], sems.at[i]) for i in range(4)]
    outward = [pltpu.make_async_copy(held.at[i], outs[i], sems.at[4 + i]) for i in range(4)]
    for copy in inward:
        copy.start()
    for i in range(4):
        inward[i].wait()
        outward[i].start()
    for copy in outward:
        copy.wait()


def shard(dtype=BF16):
    return pltpu.VMEM((NB * 16, HALF), dtype)


def scratch():
    blocks = pltpu.VMEM((NB, 16, HALF), BF16)
    exchange = (NZ, 2, 16, HALF)
    copies = 16 * NEAR + 4 * (4 * FAR - 2) + (NEAR + 2 * FAR + 1) * 3 + 24 + 4
    far = [
        [pltpu.VMEM((2, far_count(sign, side), NY, 16, HALF), BF16) for side in range(2)]
        for sign in SIGNS
    ]
    raw = [
        [pltpu.VMEM(((far_count(sign, side) + 1) * HALF, HALF), BF16) for side in range(2)]
        for sign in SIGNS
    ]
    hot_far = [
        [pltpu.VMEM((NB * 16, (far_count(sign, side) + 1) * HALF), BF16) for side in range(2)]
        for sign in SIGNS
    ]
    return {
        "common": [shard(F32)] * 2,
        "innov": [shard(F32)] * 2,
        "grad": [shard(F32)] * 2,
        "other": [shard(F32)] * 2,
        "own": [blocks] * 2,
        "dense": [[[blocks] * 2 for _ in range(NEAR)] for _ in range(2)],
        "far_send": far,
        "far": far,
        "ysend": pltpu.VMEM((2, NY - 1) + exchange, BF16),
        "g": pltpu.VMEM((2, NY) + exchange, BF16),
        "obs": pltpu.VMEM((2, EXT, 2 * EXT), BF16),
        "obs_o": pltpu.VMEM((2, EXT, 2 * EXT), BF16),
        "order": pltpu.VMEM((EXT, EXT), BF16),
        "weight": pltpu.VMEM((2, EXT, EXT), BF16),
        "hot": [shard()] * 2,
        "hot_far": hot_far,
        "wide": [pltpu.VMEM((2 * EXT, HALF), F32)] * 2,
        "back": pltpu.VMEM((2, NY - 1, 2, NZ, 16, HALF), BF16),
        "q": pltpu.VMEM((2, NY, 2, NZ, 16, HALF), BF16),
        "raw_send": raw,
        "raw": raw,
        "sum_send": [[[shard()] * 2 for _ in range(NEAR)] for _ in range(2)],
        "sum": [[[shard()] * 2 for _ in range(NEAR)] for _ in range(2)],
        "add": [[pltpu.VMEM((NB * 16, 2 * HALF), F32)] * 2 for _ in range(NEAR - 1)],
        "send": pltpu.SemaphoreType.DMA((copies,)),
        "recv": pltpu.SemaphoreType.DMA((copies,)),
        "local_sem": pltpu.SemaphoreType.DMA((1,)),
    }


def per_device(
    observed,
    common_left,
    common_right,
    innov_left,
    innov_right,
    tile_block_pairs,
    live,
    row_mask,
    col_mask,
):
    rows, width = common_left.shape[0], common_left.shape[2]
    vmem = pl.BlockSpec(memory_space=pltpu.VMEM)
    smem = pl.BlockSpec(memory_space=pltpu.SMEM)
    outs = pl.pallas_call(
        kernel,
        out_shape=[jax.ShapeDtypeStruct((2 * rows, HALF), F32)] * 4,
        in_specs=[smem, smem, pl.BlockSpec(memory_space=pl.ANY)] + [vmem] * 6,
        out_specs=[vmem] * 4,
        scratch_shapes=[scratch()],
        compiler_params=pltpu.CompilerParams(
            collective_id=0, has_side_effects=True, vmem_limit_bytes=56 * 1024 * 1024
        ),
    )(
        tile_block_pairs.transpose(0, 2, 3, 1),
        live.transpose(0, 2, 1),
        observed,
        common_left.reshape(rows, width),
        common_right.reshape(rows, width),
        innov_left.reshape(rows, width),
        innov_right.reshape(rows, width),
        row_mask.reshape(2, EXT),
        col_mask.reshape(2, EXT),
    )
    outs = pl.pallas_call(
        hand_over,
        out_shape=[jax.ShapeDtypeStruct((2 * rows, HALF), F32)] * 4,
        in_specs=[pl.BlockSpec(memory_space=pl.ANY)] * 4,
        out_specs=[pl.BlockSpec(memory_space=pl.ANY)] * 4,
        scratch_shapes=[pltpu.VMEM((4, 2 * rows, HALF), F32), pltpu.SemaphoreType.DMA((8,))],
        compiler_params=pltpu.CompilerParams(vmem_limit_bytes=56 * 1024 * 1024),
    )(*outs)
    return (
        outs[0].reshape(rows, 1, width),
        outs[1].reshape(rows, 1, width),
        outs[2].reshape(1, rows, 1, width),
        outs[3].reshape(1, rows, 1, width),
    )


def solution(mesh):
    placed = (
        P("vintage", "tile", "freq", None, None),
        P("freq", "tile", None),
        P("freq", "tile", None),
        P("vintage", "freq", "tile", None),
        P("vintage", "freq", "tile", None),
        P(None, None, "freq", None),
        P(None, None, "freq"),
        P("vintage", "tile", "freq", None),
        P("vintage", "tile", "freq", None),
    )
    return jax.shard_map(
        per_device,
        mesh=mesh,
        in_specs=placed,
        out_specs=(
            P("freq", "tile", None),
            P("freq", "tile", None),
            P("vintage", "freq", "tile", None),
            P("vintage", "freq", "tile", None),
        ),
        check_vma=False,
    )
```

```python
import jax
import jax.numpy as jnp
from jax import lax
from jax.experimental import pallas as pl
from jax.experimental.pallas import tpu as pltpu
from jax.sharding import PartitionSpec as P

MESH = pl.DeviceIdType.MESH
BF16, F32 = jnp.bfloat16, jnp.float32

step_size = 8.0
shrink = 0.5

NZ, NY = 16, 4
EXT = 512
NB = 32
HALF = 128
NEAR = 2
FAR = NZ // 2 - NEAR
SIGNS = (1, -1)
HALVES = (pl.ds(0, NB // 2), pl.ds(NB // 2, NB // 2))
ROWS = (pl.ds(0, NB * 8), pl.ds(NB * 8, NB * 8))


def place(rel):
    if abs(rel) == NZ // 2:
        return 0
    far = 2 * (NZ // 2 - abs(rel))
    return far - 1 if rel >= 0 else far


def far_count(sign, side):
    return FAR if (sign > 0) == (side == 0) else FAR - 1


def dot(a, b, ca=1, cb=0):
    return lax.dot_general(a, b, (((ca,), (cb,)), ((), ())), preferred_element_type=F32)


def kernel(
    pairs,
    live,
    observed,
    common_left,
    common_right,
    innov_left,
    innov_right,
    row_mask,
    col_mask,
    out_common_left,
    out_common_right,
    out_innov_left,
    out_innov_right,
    s,
):
    v = lax.axis_index("vintage")
    t = lax.axis_index("tile")
    z, y = t // NY, t % NY

    def along_z(d):
        return {"tile": lax.rem(z + d + NZ, NZ) * NY + y}

    def along_y(d):
        return {"tile": z * NY + lax.rem(y + d + NY, NY)}

    partner = {"vintage": 1 - v}

    barrier = pltpu.get_barrier_semaphore()
    peers = [along_z(sg * e) for e in range(1, max(FAR, 1) + 1) for sg in SIGNS]
    peers += [along_y(k) for k in range(1, NY)] + [partner]
    for peer in peers:
        pl.semaphore_signal(barrier, inc=1, device_id=peer, device_id_type=MESH)

    load_obs = pltpu.make_async_copy(observed.at[0, 0], s["obs"], s["local_sem"].at[0])
    load_obs.start()

    started, gone = [], set()

    def leave(copies):
        for copy in copies:
            copy.wait_send()
            gone.add(id(copy))

    def send(src, dst, dev):
        i = len(started)
        copy = pltpu.make_async_remote_copy(
            src_ref=src,
            dst_ref=dst,
            send_sem=s["send"].at[i],
            recv_sem=s["recv"].at[i],
            device_id=dev,
            device_id_type=MESH,
        )
        copy.start()
        started.append(copy)
        return copy

    def pick(rel, k, slot, side):
        owner = lax.rem(z + rel + NZ, NZ) * NY + lax.rem(y + k, NY)
        return pairs[v, slot, side, owner]

    commons = (common_left, common_right)
    innovs = (innov_left, innov_right)
    for side in range(2):
        for src, dst in ((commons[side], s["common"][side]), (innovs[side], s["innov"][side])):
            x = src[...].astype(F32)
            dst[pl.ds(0, NB * 8, 2), :] = x[:, :HALF]
            dst[pl.ds(1, NB * 8, 2), :] = x[:, HALF:]
        joined = (s["common"][side][...] + s["innov"][side][...]).astype(BF16)
        s["own"][side][...] = joined.reshape(NB, 16, HALF)

    pl.semaphore_wait(barrier, len(peers))

    dense = {}

    def first_hop(side):
        for c, blocks in enumerate(HALVES):
            for g, sign in enumerate(SIGNS):
                dense[g, 1, side, c] = send(
                    s["own"][side].at[blocks], s["dense"][g][0][side].at[blocks], along_z(sign)
                )

    first_hop(0)

    def choose(bufs, o):
        for k in range(NY):
            for side in range(2):
                for slot in range(2):
                    piece = bufs[side][pick(0, k, slot, side)]
                    if k == 0:
                        s["g"][slot, 0, o, side] = piece
                    else:
                        s["ysend"][slot, k - 1, o, side] = piece

    def spread(slots, o0, n):
        return [
            send(
                s["ysend"].at[slots, k - 1, pl.ds(o0, n)],
                s["g"].at[slots, k, pl.ds(o0, n)],
                along_y(k),
            )
            for k in range(1, NY)
        ]

    both_slots = pl.ds(0, 2)

    def build_order():
        row = lax.broadcasted_iota(jnp.int32, (EXT, HALF), 0)
        lane = lax.broadcasted_iota(jnp.int32, (EXT, HALF), 1)
        k, o, j = row >> 7, (row >> 3) & 15, row & 7
        dist = NZ // 2 - ((o + 1) >> 1)
        rel = jnp.where((o & 1) == 1, dist, -dist)
        target = 64 * j + ((z + rel + NZ) & (NZ - 1)) * NY + ((y - k + NY) & (NY - 1))
        for c in range(EXT // HALF):
            s["order"][:, c * HALF : (c + 1) * HALF] = jnp.where(
                target == lane + c * HALF, 1.0, 0.0
            ).astype(BF16)

    def order_tile(slot):
        order = s["order"][...]
        turned = dot(order, s["obs"][slot]).astype(BF16)
        for h in range(2):
            cols = slice(h * EXT, (h + 1) * EXT)
            s["obs_o"][slot, :, cols] = dot(turned[:, cols], order, 1, 1).astype(BF16)

    def order_masks(slot):
        order = s["order"][...]
        rows = jnp.broadcast_to(row_mask[slot : slot + 1, :].astype(F32), (HALF, EXT)).astype(BF16)
        cols = jnp.broadcast_to(col_mask[slot : slot + 1, :].astype(F32), (16, EXT)).astype(BF16)
        by_row = dot(order, rows, 1, 1)
        by_col = dot(cols, order, 1, 1)[0:1, :]
        weight = jnp.concatenate([by_row] * (EXT // HALF), axis=1) * by_col
        s["weight"][slot] = (weight * live[v, slot, t].astype(F32)).astype(BF16)

    def one_hot(rel, side):
        row = lax.broadcasted_iota(jnp.int32, (NB * 16, HALF), 0)
        lane = lax.broadcasted_iota(jnp.int32, (1, HALF), 1)
        target = jnp.zeros((1, HALF), jnp.int32)
        for slot in range(2):
            for k in range(NY):
                target = jnp.where(
                    (lane >> 4) == slot * NY + k, pick(rel, k, slot, side), target
                )
        return jnp.where(row == target * 16 + (lane & 15), 1.0, 0.0).astype(BF16)

    def build_own_hot():
        for side in range(2):
            hot = one_hot(0, side)
            s["hot"][side][...] = hot
            for g in range(2):
                s["hot_far"][g][side][:, :HALF] = hot

    def build_far_hot(g):
        sign = SIGNS[g]
        for side in range(2):
            for e in range(1, far_count(sign, side) + 1):
                s["hot_far"][g][side][:, e * HALF : (e + 1) * HALF] = one_hot(-sign * e, side)

    choose(s["own"], place(0))
    near = spread(both_slots, place(0), 1)
    build_order()
    leave([dense[g, 1, 0, c] for c in range(2) for g in range(2)])
    first_hop(1)

    picks = {}

    def stage_far(g, side, slot):
        here = s["dense"][g][NEAR - 1][side]
        for e in range(far_count(SIGNS[g], side), 0, -1):
            for k in range(NY):
                s["far_send"][g][side][slot, e - 1, k] = here[pick(SIGNS[g] * e, k, slot, side)]

    def send_far(side, slot):
        for e in range(FAR, 0, -1):
            for g, sign in enumerate(SIGNS):
                if e <= far_count(sign, side):
                    picks[g, e, side, slot] = send(
                        s["far_send"][g][side].at[slot, e - 1],
                        s["far"][g][side].at[slot, e - 1],
                        along_z(sign * e),
                    )

    for h in range(1, NEAR + 1):
        for side in range(2):
            for c, blocks in enumerate(HALVES):
                for g, sign in enumerate(SIGNS):
                    dense[g, h, side, c].wait_recv()
                    if h < NEAR:
                        dense[g, h + 1, side, c] = send(
                            s["dense"][g][h - 1][side].at[blocks],
                            s["dense"][g][h][side].at[blocks],
                            along_z(sign),
                        )
            if h == NEAR:
                for g in range(2):
                    stage_far(g, side, 0)
                send_far(side, 0)
        for g, sign in enumerate(SIGNS):
            choose(s["dense"][g][h - 1], place(-sign * h))
        near += spread(both_slots, place(h), 2)
    for side in range(2):
        for g in range(2):
            stage_far(g, side, 1)
    load_obs.wait()
    order_tile(0)
    leave([picks[key] for key in picks if key[3] == 0])
    for side in range(2):
        send_far(side, 1)
    order_masks(0)
    order_tile(1)
    order_masks(1)

    def far_in(slot):
        copies = []
        for e in range(FAR, 0, -1):
            d = NEAR + e
            for g, sign in enumerate(SIGNS):
                for side in range(2):
                    if e <= far_count(sign, side):
                        picks[g, e, side, slot].wait_recv()
                        o = place(-sign * d)
                        s["g"][slot, 0, o, side] = s["far"][g][side][slot, e - 1, 0]
                        for k in range(1, NY):
                            s["ysend"][slot, k - 1, o, side] = s["far"][g][side][slot, e - 1, k]
            copies += spread(slot, place(d), 1 if d == NZ // 2 else 2)
        return copies

    def parts(side, slot):
        x = s["g"][slot, :, :, side].reshape(2 * EXT, HALF).astype(F32)
        s["wide"][side][...] = x
        real = s["wide"][side][pl.ds(0, EXT, 2), :].astype(BF16)
        imag = s["wide"][side][pl.ds(1, EXT, 2), :].astype(BF16)
        return real, imag

    def keep(delta, side, slot):
        s["wide"][side][pl.ds(0, EXT, 2), :] = delta[:, :HALF]
        s["wide"][side][pl.ds(1, EXT, 2), :] = delta[:, HALF:]
        pieces = s["wide"][side][...].astype(BF16).reshape(NY, NZ, 16, HALF)
        s["q"][slot, 0, side] = pieces[0]
        for k in range(1, NY):
            s["back"][slot, k - 1, side] = pieces[k]

    back = {}

    def give_back(slot, i, sides, o0, n):
        for k in (2, 1, 3):
            back[slot, i, k] = send(
                s["back"].at[slot, k - 1, sides, pl.ds(o0, n)],
                s["q"].at[slot, k, sides, pl.ds(o0, n)],
                along_y(-k),
            )

    scale = 1.0 / EXT

    def tile(slot):
        a_re, a_im = parts(0, slot)
        b_re, b_im = parts(1, slot)
        a = jnp.concatenate([a_re, a_im], axis=1)
        s_re = jnp.concatenate([b_re, -b_im], axis=1)
        s_im = jnp.concatenate([b_im, b_re], axis=1)
        t_re = jnp.concatenate([a_re, -a_im], axis=1)
        t_im = jnp.concatenate([a_im, a_re], axis=1)
        weight = s["weight"][slot].astype(F32)
        m_re = (weight * (dot(a, s_re, 1, 1) - s["obs_o"][slot, :, :EXT].astype(F32))).astype(BF16)
        m_im = (weight * (dot(a, s_im, 1, 1) - s["obs_o"][slot, :, EXT:].astype(F32))).astype(BF16)
        keep((dot(m_re, s_re) + dot(m_im, s_im)) * scale, 0, slot)
        give_back(slot, 0, 0, 0, 2 * FAR - 1)
        keep((dot(m_re, t_re, 0, 0) + dot(m_im, t_im, 0, 0)) * scale, 1, slot)
        give_back(slot, 1, 1, 0, 2 * FAR - 1)
        give_back(slot, 2, pl.ds(0, 2), 2 * FAR - 1, 4)
        give_back(slot, 3, pl.ds(0, 2), 2 * FAR + 3, 2 * NEAR - 3)

    def arrived(slot, i):
        for k in range(1, NY):
            back[slot, i, k].wait_recv()

    def own_picks(rel, side):
        return s["q"][:, :, side, place(rel)].reshape(HALF, HALF)

    raw = {}

    def far_out(slot):
        for side in range(2):
            arrived(slot, side)
            for e in range(FAR, 0, -1):
                for g, sign in enumerate(SIGNS):
                    if e <= far_count(sign, side):
                        rows = pl.ds(e * HALF + slot * (HALF // 2), HALF // 2)
                        mine = s["q"][slot, :, side, place(sign * (NEAR + e))]
                        s["raw_send"][g][side][rows, :] = mine.reshape(HALF // 2, HALF)
                        raw[g, e, side, slot] = send(
                            s["raw_send"][g][side].at[rows],
                            s["raw"][g][side].at[rows],
                            along_z(sign * e),
                        )

    early = far_in(0)
    for copy in near + early:
        copy.wait_recv()
    tile(0)
    build_own_hot()
    late = far_in(1)
    far_out(0)
    for copy in late:
        copy.wait_recv()
    tile(1)
    far_out(1)
    for g in range(2):
        build_far_hot(g)
    for slot in range(2):
        arrived(slot, 2)
    for g, sign in enumerate(SIGNS):
        for side in range(2):
            s["raw"][g][side][0:HALF, :] = own_picks(sign * NEAR, side)

    def own_sums(h):
        for side in range(2):
            both = jnp.concatenate([own_picks(h, side), own_picks(-h, side)], axis=1)
            s["add"][h - 1][side][...] = dot(s["hot"][side][...], both)

    own_sums(NEAR - 1)
    chain = {}

    def pass_on(g, h, side, c):
        chain[g, h, side, c] = send(
            s["sum_send"][g][h][side].at[ROWS[c]], s["sum"][g][h][side].at[ROWS[c]], along_z(SIGNS[g])
        )

    for side in range(2):
        for g, sign in enumerate(SIGNS):
            for slot in range(2):
                for e in range(far_count(sign, side), 0, -1):
                    raw[g, e, side, slot].wait_recv()
        for c, rows in enumerate(ROWS):
            for g, sign in enumerate(SIGNS):
                depth = (far_count(sign, side) + 1) * HALF
                total = dot(s["hot_far"][g][side][rows, :depth], s["raw"][g][side][0:depth, :])
                s["sum_send"][g][NEAR - 1][side][rows, :] = total.astype(BF16)
                if side == 1:
                    leave([chain[g, NEAR - 1, 0, c]])
                pass_on(g, NEAR - 1, side, c)
    for slot in range(2):
        arrived(slot, 3)
    for h in range(NEAR - 2, 0, -1):
        own_sums(h)
    for side in range(2):
        s["grad"][side][...] = dot(s["hot"][side][...], own_picks(0, side))
    for h in range(NEAR - 1, 0, -1):
        for side in range(2):
            for c, rows in enumerate(ROWS):
                for g in range(2):
                    chain[g, h, side, c].wait_recv()
                    total = s["sum"][g][h][side][rows, :].astype(F32)
                    total = total + s["add"][h - 1][side][rows, g * HALF : (g + 1) * HALF]
                    s["sum_send"][g][h - 1][side][rows, :] = total.astype(BF16)
                    pass_on(g, h - 1, side, c)
    swap = {}
    for side in range(2):
        for c, rows in enumerate(ROWS):
            for g in range(2):
                chain[g, 0, side, c].wait_recv()
            s["grad"][side][rows, :] = (
                s["grad"][side][rows, :]
                + s["sum"][0][0][side][rows, :].astype(F32)
                + s["sum"][1][0][side][rows, :].astype(F32)
            )
            swap[side, c] = send(s["grad"][side].at[rows], s["other"][side].at[rows], partner)
        innov = s["innov"][side][...]
        out = (out_innov_left, out_innov_right)[side]
        out[...] = innov - step_size * (s["grad"][side][...] + shrink * innov)
    for side, out in enumerate((out_common_left, out_common_right)):
        for c, rows in enumerate(ROWS):
            swap[side, c].wait_recv()
            out[rows, :] = s["common"][side][rows, :] - step_size * (
                s["grad"][side][rows, :] + s["other"][side][rows, :]
            )
    leave([copy for copy in started if id(copy) not in gone])


def hand_over(*refs):
    given, outs, held, sems = refs[:4], refs[4:8], refs[8], refs[9]
    inward = [pltpu.make_async_copy(given[i], held.at[i], sems.at[i]) for i in range(4)]
    outward = [pltpu.make_async_copy(held.at[i], outs[i], sems.at[4 + i]) for i in range(4)]
    for copy in inward:
        copy.start()
    for i in range(4):
        inward[i].wait()
        outward[i].start()
    for copy in outward:
        copy.wait()


def shard(dtype=BF16):
    return pltpu.VMEM((NB * 16, HALF), dtype)


def scratch():
    blocks = pltpu.VMEM((NB, 16, HALF), BF16)
    exchange = (NZ, 2, 16, HALF)
    copies = 16 * NEAR + 4 * (4 * FAR - 2) + (NEAR + 2 * FAR + 1) * 3 + 24 + 4
    far = [
        [pltpu.VMEM((2, far_count(sign, side), NY, 16, HALF), BF16) for side in range(2)]
        for sign in SIGNS
    ]
    raw = [
        [pltpu.VMEM(((far_count(sign, side) + 1) * HALF, HALF), BF16) for side in range(2)]
        for sign in SIGNS
    ]
    hot_far = [
        [pltpu.VMEM((NB * 16, (far_count(sign, side) + 1) * HALF), BF16) for side in range(2)]
        for sign in SIGNS
    ]
    return {
        "common": [shard(F32)] * 2,
        "innov": [shard(F32)] * 2,
        "grad": [shard(F32)] * 2,
        "other": [shard(F32)] * 2,
        "own": [blocks] * 2,
        "dense": [[[blocks] * 2 for _ in range(NEAR)] for _ in range(2)],
        "far_send": far,
        "far": far,
        "ysend": pltpu.VMEM((2, NY - 1) + exchange, BF16),
        "g": pltpu.VMEM((2, NY) + exchange, BF16),
        "obs": pltpu.VMEM((2, EXT, 2 * EXT), BF16),
        "obs_o": pltpu.VMEM((2, EXT, 2 * EXT), BF16),
        "order": pltpu.VMEM((EXT, EXT), BF16),
        "weight": pltpu.VMEM((2, EXT, EXT), BF16),
        "hot": [shard()] * 2,
        "hot_far": hot_far,
        "wide": [pltpu.VMEM((2 * EXT, HALF), F32)] * 2,
        "back": pltpu.VMEM((2, NY - 1, 2, NZ, 16, HALF), BF16),
        "q": pltpu.VMEM((2, NY, 2, NZ, 16, HALF), BF16),
        "raw_send": raw,
        "raw": raw,
        "sum_send": [[[shard()] * 2 for _ in range(NEAR)] for _ in range(2)],
        "sum": [[[shard()] * 2 for _ in range(NEAR)] for _ in range(2)],
        "add": [[pltpu.VMEM((NB * 16, 2 * HALF), F32)] * 2 for _ in range(NEAR - 1)],
        "send": pltpu.SemaphoreType.DMA((copies,)),
        "recv": pltpu.SemaphoreType.DMA((copies,)),
        "local_sem": pltpu.SemaphoreType.DMA((1,)),
    }


def per_device(
    observed,
    common_left,
    common_right,
    innov_left,
    innov_right,
    tile_block_pairs,
    live,
    row_mask,
    col_mask,
):
    rows, width = common_left.shape[0], common_left.shape[2]
    vmem = pl.BlockSpec(memory_space=pltpu.VMEM)
    smem = pl.BlockSpec(memory_space=pltpu.SMEM)
    outs = pl.pallas_call(
        kernel,
        out_shape=[jax.ShapeDtypeStruct((2 * rows, HALF), F32)] * 4,
        in_specs=[smem, smem, pl.BlockSpec(memory_space=pl.ANY)] + [vmem] * 6,
        out_specs=[vmem] * 4,
        scratch_shapes=[scratch()],
        compiler_params=pltpu.CompilerParams(
            collective_id=0, has_side_effects=True, vmem_limit_bytes=56 * 1024 * 1024
        ),
    )(
        tile_block_pairs.transpose(0, 2, 3, 1),
        live.transpose(0, 2, 1),
        observed,
        common_left.reshape(rows, width),
        common_right.reshape(rows, width),
        innov_left.reshape(rows, width),
        innov_right.reshape(rows, width),
        row_mask.reshape(2, EXT),
        col_mask.reshape(2, EXT),
    )
    outs = pl.pallas_call(
        hand_over,
        out_shape=[jax.ShapeDtypeStruct((2 * rows, HALF), F32)] * 4,
        in_specs=[pl.BlockSpec(memory_space=pl.ANY)] * 4,
        out_specs=[pl.BlockSpec(memory_space=pl.ANY)] * 4,
        scratch_shapes=[pltpu.VMEM((4, 2 * rows, HALF), F32), pltpu.SemaphoreType.DMA((8,))],
        compiler_params=pltpu.CompilerParams(vmem_limit_bytes=56 * 1024 * 1024),
    )(*outs)
    return (
        outs[0].reshape(rows, 1, width),
        outs[1].reshape(rows, 1, width),
        outs[2].reshape(1, rows, 1, width),
        outs[3].reshape(1, rows, 1, width),
    )


def solution(mesh):
    placed = (
        P("vintage", "tile", "freq", None, None),
        P("freq", "tile", None),
        P("freq", "tile", None),
        P("vintage", "freq", "tile", None),
        P("vintage", "freq", "tile", None),
        P(None, None, "freq", None),
        P(None, None, "freq"),
        P("vintage", "tile", "freq", None),
        P("vintage", "tile", "freq", None),
    )
    return jax.shard_map(
        per_device,
        mesh=mesh,
        in_specs=placed,
        out_specs=(
            P("freq", "tile", None),
            P("freq", "tile", None),
            P("vintage", "freq", "tile", None),
            P("vintage", "freq", "tile", None),
        ),
        check_vma=False,
    )
```

```python
import jax
import jax.numpy as jnp
from jax import lax
from jax.experimental import pallas as pl
from jax.experimental.pallas import tpu as pltpu
from jax.sharding import PartitionSpec as P

MESH = pl.DeviceIdType.MESH
BF16, F32 = jnp.bfloat16, jnp.float32

step_size = 8.0
shrink = 0.5

NZ, NY = 16, 4
EXT = 512
NB = 32
HALF = 128
NEAR = 2
FAR = NZ // 2 - NEAR
SIGNS = (1, -1)
HALVES = (pl.ds(0, NB // 2), pl.ds(NB // 2, NB // 2))
ROWS = (pl.ds(0, NB * 8), pl.ds(NB * 8, NB * 8))


def place(rel):
    if abs(rel) == NZ // 2:
        return 0
    far = 2 * (NZ // 2 - abs(rel))
    return far - 1 if rel >= 0 else far


def far_count(sign, side):
    return FAR if (sign > 0) == (side == 0) else FAR - 1


def dot(a, b, ca=1, cb=0):
    return lax.dot_general(a, b, (((ca,), (cb,)), ((), ())), preferred_element_type=F32)


def kernel(
    pairs,
    live,
    observed,
    common_left,
    common_right,
    innov_left,
    innov_right,
    row_mask,
    col_mask,
    out_common_left,
    out_common_right,
    out_innov_left,
    out_innov_right,
    s,
):
    v = lax.axis_index("vintage")
    t = lax.axis_index("tile")
    z, y = t // NY, t % NY

    def along_z(d):
        return {"tile": lax.rem(z + d + NZ, NZ) * NY + y}

    def along_y(d):
        return {"tile": z * NY + lax.rem(y + d + NY, NY)}

    partner = {"vintage": 1 - v}

    barrier = pltpu.get_barrier_semaphore()
    peers = [along_z(sg * e) for e in range(1, max(FAR, 1) + 1) for sg in SIGNS]
    peers += [along_y(k) for k in range(1, NY)] + [partner]
    for peer in peers:
        pl.semaphore_signal(barrier, inc=1, device_id=peer, device_id_type=MESH)

    load_obs = pltpu.make_async_copy(observed.at[0, 0], s["obs"], s["local_sem"].at[0])
    load_obs.start()

    started, gone = [], set()

    def leave(copies):
        for copy in copies:
            copy.wait_send()
            gone.add(id(copy))

    def send(src, dst, dev):
        i = len(started)
        copy = pltpu.make_async_remote_copy(
            src_ref=src,
            dst_ref=dst,
            send_sem=s["send"].at[i],
            recv_sem=s["recv"].at[i],
            device_id=dev,
            device_id_type=MESH,
        )
        copy.start()
        started.append(copy)
        return copy

    def pick(rel, k, slot, side):
        owner = lax.rem(z + rel + NZ, NZ) * NY + lax.rem(y + k, NY)
        return pairs[v, slot, side, owner]

    commons = (common_left, common_right)
    innovs = (innov_left, innov_right)

    def prepare(side):
        for src, dst in ((commons[side], s["common"][side]), (innovs[side], s["innov"][side])):
            x = src[...].astype(F32)
            dst[pl.ds(0, NB * 8, 2), :] = x[:, :HALF]
            dst[pl.ds(1, NB * 8, 2), :] = x[:, HALF:]
        joined = (s["common"][side][...] + s["innov"][side][...]).astype(BF16)
        s["own"][side][...] = joined.reshape(NB, 16, HALF)

    prepare(0)
    pl.semaphore_wait(barrier, len(peers))

    dense = {}

    def first_hop(side):
        for c, blocks in enumerate(HALVES):
            for g, sign in enumerate(SIGNS):
                dense[g, 1, side, c] = send(
                    s["own"][side].at[blocks], s["dense"][g][0][side].at[blocks], along_z(sign)
                )

    first_hop(0)
    prepare(1)

    def choose(bufs, o):
        for k in range(NY):
            for side in range(2):
                for slot in range(2):
                    piece = bufs[side][pick(0, k, slot, side)]
                    if k == 0:
                        s["g"][slot, 0, o, side] = piece
                    else:
                        s["ysend"][slot, k - 1, o, side] = piece

    def spread(slots, o0, n):
        return [
            send(
                s["ysend"].at[slots, k - 1, pl.ds(o0, n)],
                s["g"].at[slots, k, pl.ds(o0, n)],
                along_y(k),
            )
            for k in range(1, NY)
        ]

    both_slots = pl.ds(0, 2)

    def build_order():
        row = lax.broadcasted_iota(jnp.int32, (EXT, HALF), 0)
        lane = lax.broadcasted_iota(jnp.int32, (EXT, HALF), 1)
        k, o, j = row >> 7, (row >> 3) & 15, row & 7
        dist = NZ // 2 - ((o + 1) >> 1)
        rel = jnp.where((o & 1) == 1, dist, -dist)
        target = 64 * j + ((z + rel + NZ) & (NZ - 1)) * NY + ((y - k + NY) & (NY - 1))
        for c in range(EXT // HALF):
            s["order"][:, c * HALF : (c + 1) * HALF] = jnp.where(
                target == lane + c * HALF, 1.0, 0.0
            ).astype(BF16)

    def order_tile(slot):
        order = s["order"][...]
        turned = dot(order, s["obs"][slot]).astype(BF16)
        for h in range(2):
            cols = slice(h * EXT, (h + 1) * EXT)
            s["obs_o"][slot, :, cols] = dot(turned[:, cols], order, 1, 1).astype(BF16)

    def order_masks(slot):
        order = s["order"][...]
        rows = jnp.broadcast_to(row_mask[slot : slot + 1, :].astype(F32), (HALF, EXT)).astype(BF16)
        cols = jnp.broadcast_to(col_mask[slot : slot + 1, :].astype(F32), (16, EXT)).astype(BF16)
        by_row = dot(order, rows, 1, 1)
        by_col = dot(cols, order, 1, 1)[0:1, :]
        weight = jnp.concatenate([by_row] * (EXT // HALF), axis=1) * by_col
        s["weight"][slot] = (weight * live[v, slot, t].astype(F32)).astype(BF16)

    def one_hot(rel, side):
        row = lax.broadcasted_iota(jnp.int32, (NB * 16, HALF), 0)
        lane = lax.broadcasted_iota(jnp.int32, (1, HALF), 1)
        target = jnp.zeros((1, HALF), jnp.int32)
        for slot in range(2):
            for k in range(NY):
                target = jnp.where(
                    (lane >> 4) == slot * NY + k, pick(rel, k, slot, side), target
                )
        return jnp.where(row == target * 16 + (lane & 15), 1.0, 0.0).astype(BF16)

    def build_own_hot():
        for side in range(2):
            hot = one_hot(0, side)
            s["hot"][side][...] = hot
            for g in range(2):
                s["hot_far"][g][side][:, :HALF] = hot

    def build_far_hot(g):
        sign = SIGNS[g]
        for side in range(2):
            for e in range(1, far_count(sign, side) + 1):
                s["hot_far"][g][side][:, e * HALF : (e + 1) * HALF] = one_hot(-sign * e, side)

    choose(s["own"], place(0))
    near = spread(both_slots, place(0), 1)
    build_order()
    leave([dense[g, 1, 0, c] for c in range(2) for g in range(2)])
    first_hop(1)

    picks = {}

    def stage_far(g, side, slot):
        here = s["dense"][g][NEAR - 1][side]
        for e in range(far_count(SIGNS[g], side), 0, -1):
            for k in range(NY):
                s["far_send"][g][side][slot, e - 1, k] = here[pick(SIGNS[g] * e, k, slot, side)]

    def send_far(side, slot):
        for e in range(FAR, 0, -1):
            for g, sign in enumerate(SIGNS):
                if e <= far_count(sign, side):
                    picks[g, e, side, slot] = send(
                        s["far_send"][g][side].at[slot, e - 1],
                        s["far"][g][side].at[slot, e - 1],
                        along_z(sign * e),
                    )

    for h in range(1, NEAR + 1):
        for side in range(2):
            for c, blocks in enumerate(HALVES):
                for g, sign in enumerate(SIGNS):
                    dense[g, h, side, c].wait_recv()
                    if h < NEAR:
                        dense[g, h + 1, side, c] = send(
                            s["dense"][g][h - 1][side].at[blocks],
                            s["dense"][g][h][side].at[blocks],
                            along_z(sign),
                        )
            if h == NEAR:
                for g in range(2):
                    stage_far(g, side, 0)
                send_far(side, 0)
        for g, sign in enumerate(SIGNS):
            choose(s["dense"][g][h - 1], place(-sign * h))
        near += spread(both_slots, place(h), 2)
    for side in range(2):
        for g in range(2):
            stage_far(g, side, 1)
    load_obs.wait()
    order_tile(0)
    order_masks(0)
    leave([picks[key] for key in picks if key[3] == 0])
    for side in range(2):
        send_far(side, 1)
    def far_in(slot):
        copies = []
        for e in range(FAR, 0, -1):
            d = NEAR + e
            for g, sign in enumerate(SIGNS):
                for side in range(2):
                    if e <= far_count(sign, side):
                        picks[g, e, side, slot].wait_recv()
                        o = place(-sign * d)
                        s["g"][slot, 0, o, side] = s["far"][g][side][slot, e - 1, 0]
                        for k in range(1, NY):
                            s["ysend"][slot, k - 1, o, side] = s["far"][g][side][slot, e - 1, k]
            copies += spread(slot, place(d), 1 if d == NZ // 2 else 2)
        return copies

    def parts(side, slot):
        x = s["g"][slot, :, :, side].reshape(2 * EXT, HALF).astype(F32)
        s["wide"][side][...] = x
        real = s["wide"][side][pl.ds(0, EXT, 2), :].astype(BF16)
        imag = s["wide"][side][pl.ds(1, EXT, 2), :].astype(BF16)
        return real, imag

    def keep(delta, side, slot):
        s["wide"][side][pl.ds(0, EXT, 2), :] = delta[:, :HALF]
        s["wide"][side][pl.ds(1, EXT, 2), :] = delta[:, HALF:]
        pieces = s["wide"][side][...].astype(BF16).reshape(NY, NZ, 16, HALF)
        s["q"][slot, 0, side] = pieces[0]
        for k in range(1, NY):
            s["back"][slot, k - 1, side] = pieces[k]

    back = {}

    def give_back(slot, i, sides, o0, n):
        for k in (2, 1, 3):
            back[slot, i, k] = send(
                s["back"].at[slot, k - 1, sides, pl.ds(o0, n)],
                s["q"].at[slot, k, sides, pl.ds(o0, n)],
                along_y(-k),
            )

    scale = 1.0 / EXT

    def tile(slot):
        a_re, a_im = parts(0, slot)
        b_re, b_im = parts(1, slot)
        a = jnp.concatenate([a_re, a_im], axis=1)
        s_re = jnp.concatenate([b_re, -b_im], axis=1)
        s_im = jnp.concatenate([b_im, b_re], axis=1)
        t_re = jnp.concatenate([a_re, -a_im], axis=1)
        t_im = jnp.concatenate([a_im, a_re], axis=1)
        weight = s["weight"][slot].astype(F32)
        m_re = (weight * (dot(a, s_re, 1, 1) - s["obs_o"][slot, :, :EXT].astype(F32))).astype(BF16)
        m_im = (weight * (dot(a, s_im, 1, 1) - s["obs_o"][slot, :, EXT:].astype(F32))).astype(BF16)
        keep((dot(m_re, s_re) + dot(m_im, s_im)) * scale, 0, slot)
        give_back(slot, 0, 0, 0, 2 * FAR - 1)
        keep((dot(m_re, t_re, 0, 0) + dot(m_im, t_im, 0, 0)) * scale, 1, slot)
        give_back(slot, 1, 1, 0, 2 * FAR - 1)
        give_back(slot, 2, pl.ds(0, 2), 2 * FAR - 1, 4)
        give_back(slot, 3, pl.ds(0, 2), 2 * FAR + 3, 2 * NEAR - 3)

    def arrived(slot, i):
        for k in range(1, NY):
            back[slot, i, k].wait_recv()

    def own_picks(rel, side):
        return s["q"][:, :, side, place(rel)].reshape(HALF, HALF)

    raw = {}

    def far_out(slot, side):
        arrived(slot, side)
        for e in range(FAR, 0, -1):
            for g, sign in enumerate(SIGNS):
                if e <= far_count(sign, side):
                    rows = pl.ds(e * HALF + slot * (HALF // 2), HALF // 2)
                    mine = s["q"][slot, :, side, place(sign * (NEAR + e))]
                    s["raw_send"][g][side][rows, :] = mine.reshape(HALF // 2, HALF)
                    raw[g, e, side, slot] = send(
                        s["raw_send"][g][side].at[rows], s["raw"][g][side].at[rows], along_z(sign * e)
                    )

    early = far_in(0)
    order_tile(1)
    order_masks(1)
    for copy in near + early:
        copy.wait_recv()
    tile(0)
    build_own_hot()
    far_out(0, 0)
    late = far_in(1)
    far_out(0, 1)
    for copy in late:
        copy.wait_recv()
    tile(1)
    far_out(1, 0)
    far_out(1, 1)
    for g in range(2):
        build_far_hot(g)
    for slot in range(2):
        arrived(slot, 2)
    for g, sign in enumerate(SIGNS):
        for side in range(2):
            s["raw"][g][side][0:HALF, :] = own_picks(sign * NEAR, side)

    def own_sums(h):
        for side in range(2):
            both = jnp.concatenate([own_picks(h, side), own_picks(-h, side)], axis=1)
            s["add"][h - 1][side][...] = dot(s["hot"][side][...], both)

    own_sums(NEAR - 1)
    chain = {}

    def pass_on(g, h, side, c):
        chain[g, h, side, c] = send(
            s["sum_send"][g][h][side].at[ROWS[c]], s["sum"][g][h][side].at[ROWS[c]], along_z(SIGNS[g])
        )

    for side in range(2):
        for g, sign in enumerate(SIGNS):
            for slot in range(2):
                for e in range(far_count(sign, side), 0, -1):
                    raw[g, e, side, slot].wait_recv()
        for c, rows in enumerate(ROWS):
            for g, sign in enumerate(SIGNS):
                depth = (far_count(sign, side) + 1) * HALF
                total = dot(s["hot_far"][g][side][rows, :depth], s["raw"][g][side][0:depth, :])
                s["sum_send"][g][NEAR - 1][side][rows, :] = total.astype(BF16)
                if side == 1:
                    leave([chain[g, NEAR - 1, 0, c]])
                pass_on(g, NEAR - 1, side, c)
    for slot in range(2):
        arrived(slot, 3)
    for h in range(NEAR - 2, 0, -1):
        own_sums(h)
    for side in range(2):
        s["grad"][side][...] = dot(s["hot"][side][...], own_picks(0, side))
    for h in range(NEAR - 1, 0, -1):
        for side in range(2):
            for c, rows in enumerate(ROWS):
                for g in range(2):
                    chain[g, h, side, c].wait_recv()
                    total = s["sum"][g][h][side][rows, :].astype(F32)
                    total = total + s["add"][h - 1][side][rows, g * HALF : (g + 1) * HALF]
                    s["sum_send"][g][h - 1][side][rows, :] = total.astype(BF16)
                    pass_on(g, h - 1, side, c)
    swap = {}
    for side in range(2):
        for c, rows in enumerate(ROWS):
            for g in range(2):
                chain[g, 0, side, c].wait_recv()
            s["grad"][side][rows, :] = (
                s["grad"][side][rows, :]
                + s["sum"][0][0][side][rows, :].astype(F32)
                + s["sum"][1][0][side][rows, :].astype(F32)
            )
            swap[side, c] = send(s["grad"][side].at[rows], s["other"][side].at[rows], partner)
        innov = s["innov"][side][...]
        out = (out_innov_left, out_innov_right)[side]
        out[...] = innov - step_size * (s["grad"][side][...] + shrink * innov)
    for side, out in enumerate((out_common_left, out_common_right)):
        for c, rows in enumerate(ROWS):
            swap[side, c].wait_recv()
            out[rows, :] = s["common"][side][rows, :] - step_size * (
                s["grad"][side][rows, :] + s["other"][side][rows, :]
            )
    leave([copy for copy in started if id(copy) not in gone])


def hand_over(*refs):
    given, outs, held, sems = refs[:4], refs[4:8], refs[8], refs[9]
    inward = [pltpu.make_async_copy(given[i], held.at[i], sems.at[i]) for i in range(4)]
    outward = [pltpu.make_async_copy(held.at[i], outs[i], sems.at[4 + i]) for i in range(4)]
    for copy in inward:
        copy.start()
    for i in range(4):
        inward[i].wait()
        outward[i].start()
    for copy in outward:
        copy.wait()


def shard(dtype=BF16):
    return pltpu.VMEM((NB * 16, HALF), dtype)


def scratch():
    blocks = pltpu.VMEM((NB, 16, HALF), BF16)
    exchange = (NZ, 2, 16, HALF)
    copies = 16 * NEAR + 4 * (4 * FAR - 2) + (NEAR + 2 * FAR + 1) * 3 + 24 + 4
    far = [
        [pltpu.VMEM((2, far_count(sign, side), NY, 16, HALF), BF16) for side in range(2)]
        for sign in SIGNS
    ]
    raw = [
        [pltpu.VMEM(((far_count(sign, side) + 1) * HALF, HALF), BF16) for side in range(2)]
        for sign in SIGNS
    ]
    hot_far = [
        [pltpu.VMEM((NB * 16, (far_count(sign, side) + 1) * HALF), BF16) for side in range(2)]
        for sign in SIGNS
    ]
    return {
        "common": [shard(F32)] * 2,
        "innov": [shard(F32)] * 2,
        "grad": [shard(F32)] * 2,
        "other": [shard(F32)] * 2,
        "own": [blocks] * 2,
        "dense": [[[blocks] * 2 for _ in range(NEAR)] for _ in range(2)],
        "far_send": far,
        "far": far,
        "ysend": pltpu.VMEM((2, NY - 1) + exchange, BF16),
        "g": pltpu.VMEM((2, NY) + exchange, BF16),
        "obs": pltpu.VMEM((2, EXT, 2 * EXT), BF16),
        "obs_o": pltpu.VMEM((2, EXT, 2 * EXT), BF16),
        "order": pltpu.VMEM((EXT, EXT), BF16),
        "weight": pltpu.VMEM((2, EXT, EXT), BF16),
        "hot": [shard()] * 2,
        "hot_far": hot_far,
        "wide": [pltpu.VMEM((2 * EXT, HALF), F32)] * 2,
        "back": pltpu.VMEM((2, NY - 1, 2, NZ, 16, HALF), BF16),
        "q": pltpu.VMEM((2, NY, 2, NZ, 16, HALF), BF16),
        "raw_send": raw,
        "raw": raw,
        "sum_send": [[[shard()] * 2 for _ in range(NEAR)] for _ in range(2)],
        "sum": [[[shard()] * 2 for _ in range(NEAR)] for _ in range(2)],
        "add": [[pltpu.VMEM((NB * 16, 2 * HALF), F32)] * 2 for _ in range(NEAR - 1)],
        "send": pltpu.SemaphoreType.DMA((copies,)),
        "recv": pltpu.SemaphoreType.DMA((copies,)),
        "local_sem": pltpu.SemaphoreType.DMA((1,)),
    }


def per_device(
    observed,
    common_left,
    common_right,
    innov_left,
    innov_right,
    tile_block_pairs,
    live,
    row_mask,
    col_mask,
):
    rows, width = common_left.shape[0], common_left.shape[2]
    vmem = pl.BlockSpec(memory_space=pltpu.VMEM)
    smem = pl.BlockSpec(memory_space=pltpu.SMEM)
    outs = pl.pallas_call(
        kernel,
        out_shape=[jax.ShapeDtypeStruct((2 * rows, HALF), F32)] * 4,
        in_specs=[smem, smem, pl.BlockSpec(memory_space=pl.ANY)] + [vmem] * 6,
        out_specs=[vmem] * 4,
        scratch_shapes=[scratch()],
        compiler_params=pltpu.CompilerParams(
            collective_id=0, has_side_effects=True, vmem_limit_bytes=56 * 1024 * 1024
        ),
    )(
        tile_block_pairs.transpose(0, 2, 3, 1),
        live.transpose(0, 2, 1),
        observed,
        common_left.reshape(rows, width),
        common_right.reshape(rows, width),
        innov_left.reshape(rows, width),
        innov_right.reshape(rows, width),
        row_mask.reshape(2, EXT),
        col_mask.reshape(2, EXT),
    )
    outs = pl.pallas_call(
        hand_over,
        out_shape=[jax.ShapeDtypeStruct((2 * rows, HALF), F32)] * 4,
        in_specs=[pl.BlockSpec(memory_space=pl.ANY)] * 4,
        out_specs=[pl.BlockSpec(memory_space=pl.ANY)] * 4,
        scratch_shapes=[pltpu.VMEM((4, 2 * rows, HALF), F32), pltpu.SemaphoreType.DMA((8,))],
        compiler_params=pltpu.CompilerParams(vmem_limit_bytes=56 * 1024 * 1024),
    )(*outs)
    return (
        outs[0].reshape(rows, 1, width),
        outs[1].reshape(rows, 1, width),
        outs[2].reshape(1, rows, 1, width),
        outs[3].reshape(1, rows, 1, width),
    )


def solution(mesh):
    placed = (
        P("vintage", "tile", "freq", None, None),
        P("freq", "tile", None),
        P("freq", "tile", None),
        P("vintage", "freq", "tile", None),
        P("vintage", "freq", "tile", None),
        P(None, None, "freq", None),
        P(None, None, "freq"),
        P("vintage", "tile", "freq", None),
        P("vintage", "tile", "freq", None),
    )
    return jax.shard_map(
        per_device,
        mesh=mesh,
        in_specs=placed,
        out_specs=(
            P("freq", "tile", None),
            P("freq", "tile", None),
            P("vintage", "freq", "tile", None),
            P("vintage", "freq", "tile", None),
        ),
        check_vma=False,
    )
```
